256 devices in a mesh: replica: 2 (over core), dp: 4 (over y), cent: 32 (over x, z).
Axes of the slice: x: 4, y: 4, z: 8, core: 2. Of those that a mesh axis runs over, the one named last changes fastest.
Arguments:
- vectors: float32 [2048, 1024], P(('replica', 'dp')), may hold values from -6 to 6
- centroids: float32 [262144, 1024], P(('dp', 'cent')), may hold values from -6 to 6
Outputs:
- new_centroids: float32 [262144, 1024], P(('dp', 'cent'), 'replica')
The draws below stay inside these ranges and needn't reach their ends.
All inputs are finite; a program needn't handle non-finite values.
Results may differ from the reference program's by a relative error of at most 0.0022.
Values may be sent and summed in bfloat16 or wider, within the bound.
No kernel may reach another device: no remote copies, remote signals or barrier semaphores. Data moves between devices by JAX's collectives and lax.ppermute only.
A program may use at most 128 MiB of HBM per device.

```python
import math
import jax
import jax.numpy as jnp
from jax import lax

VECTOR_WIDTH = 1024
ITERS = 3
LISTS = 262144
SLAB = 1024
N_REPLICA = 2


def cluster_centres(key, clusters):
    return jax.random.normal(jax.random.fold_in(key, 101), (clusters, VECTOR_WIDTH), jnp.float32)


def draw_vectors(key, part):
    clusters = max(SLAB // 4, 4)
    centres = cluster_centres(key, clusters)
    key = jax.random.fold_in(key, 1)
    key_list = jax.random.split(key, 6)
    row_count = SLAB * N_REPLICA
    primary = jax.random.randint(key_list[0], (row_count,), 0, clusters)
    partner = (primary + jax.random.randint(key_list[1], (row_count,), 1, clusters)) % clusters
    leading_weight = jax.random.uniform(key_list[2], (row_count, 1), jnp.float32, 0.2, 1.0)
    partner_weight = jax.random.uniform(key_list[3], (row_count, 1), jnp.float32, 0.2, 1.0)
    jitter = jax.random.normal(key_list[4], (row_count, VECTOR_WIDTH), jnp.float32)
    spread = jax.random.uniform(key_list[5], (row_count, 1), jnp.float32, 0.5, 1.5)
    values = leading_weight * centres[primary] + partner_weight * centres[partner] + spread * jitter
    return jnp.clip(values, -6.0, 6.0)


def draw_centroids(key, part):
    clusters = max(SLAB // 4, 4)
    centres = cluster_centres(key, clusters)
    key = jax.random.fold_in(key, 2)
    key_list = jax.random.split(key, 4)
    owners = jnp.sort(jnp.minimum(jax.random.randint(key_list[0], (LISTS,), 0, clusters), jax.random.randint(key_list[1], (LISTS,), 0, clusters)))
    spread = jnp.exp(jax.random.uniform(key_list[2], (LISTS, 1), jnp.float32, math.log(0.5), math.log(2.0)))
    jitter = jax.random.normal(key_list[3], (LISTS, VECTOR_WIDTH), jnp.float32)
    values = centres[owners] + spread * jitter
    return jnp.clip(values, -6.0, 6.0)


def setup_inputs(seed: int = 0) -> dict:
    arg_keys = jax.random.split(jax.random.key(seed), 3)
    vectors = draw_vectors(jax.random.fold_in(arg_keys[2], 71), 0)
    centroids = draw_centroids(jax.random.fold_in(arg_keys[2], 71), 0)
    return dict(vectors=vectors, centroids=centroids)


SOFTMAX_HEAT = 0.05

def unit_rows(values):
    scale = lax.rsqrt(lax.optimization_barrier(jnp.mean(values * values, axis=-1, keepdims=True)) + 1e-06)
    return (values * scale).astype(jnp.bfloat16)

def reference(vectors, centroids):
    unit_centroids = unit_rows(centroids)
    lists_total = unit_centroids.shape[0]
    unit_vectors = unit_rows(vectors).reshape(N_REPLICA, SLAB, VECTOR_WIDTH)
    numerators = jnp.zeros((lists_total, VECTOR_WIDTH), jnp.float32)
    for member in range(N_REPLICA):
        match_scores = jnp.dot(unit_vectors[member], unit_centroids.T, preferred_element_type=jnp.float32)
        affinity_kernel = jnp.exp(match_scores / VECTOR_WIDTH / SOFTMAX_HEAT)
        row_scale = jnp.full((SLAB,), 1.0 / SLAB, jnp.float32)
        col_scale = jnp.ones((lists_total,), jnp.float32)
        for sweep in range(ITERS):
            column_totals = jnp.dot(row_scale, affinity_kernel, precision=lax.Precision.HIGHEST)
            col_scale = 1.0 / lists_total / column_totals
            row_totals = jnp.dot(affinity_kernel, col_scale, precision=lax.Precision.HIGHEST)
            row_scale = 1.0 / SLAB / row_totals
        weights = (SLAB * lists_total * row_scale[:, None] * affinity_kernel * col_scale[None, :]).astype(jnp.bfloat16)
        numerators = numerators + jnp.dot(weights.T, unit_vectors[member], preferred_element_type=jnp.float32)
    return numerators * lax.rsqrt(lax.optimization_barrier(jnp.mean(numerators * numerators, axis=-1, keepdims=True)) + 1e-06)
```

```python
import jax
import jax.numpy as jnp
from jax import lax
from jax.sharding import Mesh, PartitionSpec as P

VECTOR_WIDTH = 1024
ITERS = 3


SOFTMAX_HEAT = 0.05


def unit_rows(values):
    scale = lax.rsqrt(jnp.mean(values * values, axis=-1, keepdims=True) + 1e-06)
    return (values * scale).astype(jnp.bfloat16)


def balanced_weights(affinity_kernel, lists_total):
    members, slab_size, local_lists = affinity_kernel.shape
    row_scale = jnp.full((members, slab_size), 1.0 / slab_size, jnp.float32)
    for sweep in range(ITERS):
        column_totals = jnp.einsum(
            "sr,srk->sk", row_scale, affinity_kernel, precision=lax.Precision.HIGHEST
        )
        col_scale = 1.0 / lists_total / column_totals
        local_mass = jnp.einsum(
            "srk,sk->sr", affinity_kernel, col_scale, precision=lax.Precision.HIGHEST
        )
        row_totals = sum_over_lists(local_mass)
        row_scale = 1.0 / slab_size / row_totals
    scaled = (
        slab_size * lists_total * row_scale[:, :, None] * affinity_kernel * col_scale[:, None, :]
    )
    return scaled.astype(jnp.bfloat16)


def sum_over(partial, axes, size):
    copies = jnp.broadcast_to(partial[None], (size,) + partial.shape)
    return jnp.sum(lax.all_to_all(copies, axes, 0, 0, tiled=True), axis=0)


def sum_over_lists(local_mass):
    partial = local_mass.reshape(8, -1)
    partial = sum_over(partial, ("dp", "cx"), lax.axis_size("dp") * lax.axis_size("cx"))
    return sum_over(partial, "cz", lax.axis_size("cz")).reshape(local_mass.shape)


def score_kernel(slab_vectors, unit_centroids):
    match_scores = lax.dot_general(
        slab_vectors, unit_centroids, (((1,), (1,)), ((), ())), preferred_element_type=jnp.float32
    )
    return jnp.exp(match_scores / VECTOR_WIDTH / SOFTMAX_HEAT)


def body(vectors, centroids):
    local_unit_rows = unit_rows(vectors)
    unit_centroids = unit_rows(centroids)
    local_lists = unit_centroids.shape[0]
    lists_total = local_lists * lax.axis_size("dp") * lax.axis_size("cx") * lax.axis_size("cz")
    slab_vectors = lax.all_gather(local_unit_rows, "dp", axis=0, tiled=True)
    affinity_kernel = score_kernel(slab_vectors, unit_centroids)[None]
    weights = balanced_weights(affinity_kernel, lists_total)[0]
    partial_numer = lax.dot_general(
        weights, slab_vectors, (((0,), (0,)), ((), ())), preferred_element_type=jnp.float32
    )
    numerators = lax.psum_scatter(partial_numer, "replica", scatter_dimension=1, tiled=True)
    squares = lax.psum(jnp.sum(numerators * numerators, axis=1), "replica")
    return numerators * lax.rsqrt(squares / VECTOR_WIDTH + 1e-06)[:, None]


def solution(mesh):
    cent = mesh.shape["cent"]
    split = Mesh(
        mesh.devices.reshape(mesh.shape["replica"], mesh.shape["dp"], 4, cent // 4),
        ("replica", "dp", "cx", "cz"),
    )
    placed = (P(("replica", "dp"), None), P(("dp", "cx", "cz"), None))
    return jax.shard_map(
        body, mesh=split, in_specs=placed, out_specs=P(("dp", "cx", "cz"), "replica"), check_vma=False
    )
```

```python
import functools
import math

import jax
import jax.numpy as jnp
from jax import lax
from jax.experimental import pallas as pl
from jax.experimental.pallas import tpu as pltpu
from jax.sharding import Mesh, PartitionSpec as P

VECTOR_WIDTH = 1024
ITERS = 3
SOFTMAX_HEAT = 0.05
EXPONENT = math.log2(math.e) / SOFTMAX_HEAT / VECTOR_WIDTH

LANES = 128
GROUP_ROWS = 8
CHUNK = 256
TILE = 64
VMEM_LIMIT = 30 * 1024 * 1024
F32 = jnp.float32
BF16 = jnp.bfloat16

IN_VMEM = pl.BlockSpec(memory_space=pltpu.VMEM)


def params():
    return pltpu.CompilerParams(vmem_limit_bytes=VMEM_LIMIT)


def unit(values):
    scale = lax.rsqrt(jnp.mean(values * values, axis=-1, keepdims=True) + 1e-06)
    return (values * scale).astype(BF16)


def affinity(unit_centroids, unit_vectors):
    scores = lax.dot_general(
        unit_centroids, unit_vectors, (((1,), (1,)), ((), ())), preferred_element_type=F32
    )
    return jnp.exp2(scores * EXPONENT)


def unit_kernel(values_ref, unit_ref):
    unit_ref[...] = unit(values_ref[...])


def unit_rows(values):
    return pl.pallas_call(
        unit_kernel,
        out_shape=jax.ShapeDtypeStruct(values.shape, BF16),
        in_specs=[IN_VMEM],
        out_specs=IN_VMEM,
        compiler_params=params(),
        cost_estimate=pl.CostEstimate(flops=4 * values.size, bytes_accessed=6 * values.size, transcendentals=0),
    )(values)


def own_scores_kernel(centroids_ref, vectors_ref, unit_ref, scores_ref):
    unit_ref[...] = unit(centroids_ref[...])
    scores_ref[...] = affinity(unit_ref[...], vectors_ref[...])


def own_scores(centroids, vectors):
    lists, width = centroids.shape
    block = vectors.shape[0]
    return pl.pallas_call(
        own_scores_kernel,
        grid=(lists // CHUNK,),
        out_shape=(
            jax.ShapeDtypeStruct((lists, width), BF16),
            jax.ShapeDtypeStruct((lists, block), F32),
        ),
        in_specs=[
            pl.BlockSpec((CHUNK, width), lambda i: (i, 0)),
            pl.BlockSpec((block, width), lambda i: (0, 0)),
        ],
        out_specs=(
            pl.BlockSpec((CHUNK, width), lambda i: (i, 0)),
            pl.BlockSpec((CHUNK, block), lambda i: (i, 0)),
        ),
        compiler_params=params(),
        cost_estimate=pl.CostEstimate(
            flops=2 * lists * width * block, bytes_accessed=8 * lists * width, transcendentals=lists * block
        ),
    )(centroids, vectors)


def tile_mass(tile, row_scale, lists_total):
    totals = jnp.sum(tile * row_scale, axis=1, keepdims=True)
    col_scale = (1.0 / lists_total) / totals
    scaled = tile * col_scale
    return jnp.sum(scaled.reshape(-1, GROUP_ROWS, tile.shape[1]), axis=0)


def place_mass(mass, hops, rows_ref, copies_ref):
    row = jnp.sum(mass, axis=0, keepdims=True)
    blocks = len(hops)
    per_block = row.shape[1] // blocks // LANES
    here = lax.axis_index("dp")
    for j, hop in enumerate(hops):
        first = lax.rem(here + hop, blocks) * per_block
        for i in range(per_block):
            at = (j * per_block + i) * LANES
            rows_ref[pl.ds(first + i, 1), :] = row[:, at : at + LANES]
    copies_ref[...] = jnp.broadcast_to(rows_ref[...][None], copies_ref.shape)


def relative_row(rows_ref, hops):
    blocks = len(hops)
    per_block = rows_ref.shape[0] // blocks
    here = lax.axis_index("dp")
    parts = []
    for hop in hops:
        first = lax.rem(here + hop, blocks) * per_block
        parts += [rows_ref[pl.ds(first + i, 1), :] for i in range(per_block)]
    return jnp.concatenate(parts, axis=1)


def first_kernel(hops, lists_total, centroids_ref, own_ref, *refs):
    blocks = len(hops)
    vector_refs = refs[:blocks]
    kt_ref, slab_ref, copies_ref, mass_ref, rows_ref = refs[blocks:]
    step = pl.program_id(0)
    block = own_ref.shape[1]
    slab = block * blocks

    @pl.when(step == 0)
    def _():
        mass_ref[...] = jnp.zeros_like(mass_ref)
        for j, vector_ref in enumerate(vector_refs):
            slab_ref[pl.ds(j * block, block), :] = vector_ref[...]

    kt_ref[:, :block] = own_ref[...]
    kt_ref[:, block:] = affinity(centroids_ref[...], slab_ref[block:, :])
    row_scale = jnp.full((1, slab), 1.0 / slab, F32)
    mass = jnp.zeros(mass_ref.shape, F32)
    for t in range(CHUNK // TILE):
        mass = mass + tile_mass(kt_ref[pl.ds(t * TILE, TILE), :], row_scale, lists_total)
    mass_ref[...] += mass

    @pl.when(step == pl.num_programs(0) - 1)
    def _():
        place_mass(mass_ref[...], hops, rows_ref, copies_ref)


def first_sweep(unit_centroids, own, vectors, hops, lists_total, peers):
    lists, width = unit_centroids.shape
    block = own.shape[1]
    slab = block * len(hops)
    rows = slab // LANES
    whole = lambda shape: pl.BlockSpec(shape, lambda i: (0,) * len(shape))
    return pl.pallas_call(
        functools.partial(first_kernel, hops, lists_total),
        grid=(lists // CHUNK,),
        out_shape=(
            jax.ShapeDtypeStruct((lists, slab), F32),
            jax.ShapeDtypeStruct((slab, width), BF16),
            jax.ShapeDtypeStruct((peers, rows, LANES), F32),
        ),
        in_specs=[
            pl.BlockSpec((CHUNK, width), lambda i: (i, 0)),
            pl.BlockSpec((CHUNK, block), lambda i: (i, 0)),
        ]
        + [whole((block, width))] * len(hops),
        out_specs=(
            pl.BlockSpec((CHUNK, slab), lambda i: (i, 0)),
            whole((slab, width)),
            whole((peers, rows, LANES)),
        ),
        scratch_shapes=[pltpu.VMEM((GROUP_ROWS, slab), F32), pltpu.VMEM((rows, LANES), F32)],
        compiler_params=params(),
        cost_estimate=pl.CostEstimate(
            flops=2 * lists * width * slab, bytes_accessed=6 * lists * slab, transcendentals=lists * slab
        ),
    )(unit_centroids, own, *vectors)


def row_scale_of(received_ref, rows_ref, hops):
    totals = jnp.sum(received_ref[...], axis=0)
    rows_ref[...] = (1.0 / (totals.shape[0] * totals.shape[1])) / totals
    return relative_row(rows_ref, hops)


def sweep_kernel(hops, lists_total, received_ref, kt_ref, copies_ref, mass_ref, rows_ref, scale_ref):
    step = pl.program_id(0)

    @pl.when(step == 0)
    def _():
        mass_ref[...] = jnp.zeros_like(mass_ref)
        scale_ref[...] = row_scale_of(received_ref, rows_ref, hops)

    row_scale = scale_ref[...]
    mass = jnp.zeros(mass_ref.shape, F32)
    for t in range(CHUNK // TILE):
        mass = mass + tile_mass(kt_ref[pl.ds(t * TILE, TILE), :], row_scale, lists_total)
    mass_ref[...] += mass

    @pl.when(step == pl.num_programs(0) - 1)
    def _():
        place_mass(mass_ref[...], hops, rows_ref, copies_ref)


def next_sweep(received, kt, hops, lists_total, peers):
    lists, slab = kt.shape
    rows = slab // LANES
    return pl.pallas_call(
        functools.partial(sweep_kernel, hops, lists_total),
        grid=(lists // CHUNK,),
        out_shape=jax.ShapeDtypeStruct((peers, rows, LANES), F32),
        in_specs=[
            pl.BlockSpec(received.shape, lambda i: (0, 0, 0)),
            pl.BlockSpec((CHUNK, slab), lambda i: (i, 0)),
        ],
        out_specs=pl.BlockSpec((peers, rows, LANES), lambda i: (0, 0, 0)),
        scratch_shapes=[
            pltpu.VMEM((GROUP_ROWS, slab), F32),
            pltpu.VMEM((rows, LANES), F32),
            pltpu.VMEM((1, slab), F32),
        ],
        compiler_params=params(),
        cost_estimate=pl.CostEstimate(flops=4 * lists * slab, bytes_accessed=4 * lists * slab, transcendentals=0),
    )(received, kt)


def update_kernel(hops, lists_total, before_ref, received_ref, kt_ref, slab_ref, out_ref, rows_ref, before_scale, scale):
    @pl.when(pl.program_id(0) == 0)
    def _():
        before_scale[...] = row_scale_of(before_ref, rows_ref, hops)
        scale[...] = row_scale_of(received_ref, rows_ref, hops) * (scale.shape[1] * lists_total)

    kt = kt_ref[...]
    col_scale = (1.0 / lists_total) / jnp.sum(kt * before_scale[...], axis=1, keepdims=True)
    weights = (scale[...] * kt * col_scale).astype(BF16)
    out_ref[...] = jnp.dot(weights, slab_ref[...], preferred_element_type=F32)


def update(before, received, kt, slab_vectors, hops, lists_total):
    lists, slab = kt.shape
    width = slab_vectors.shape[1]
    rows = slab // LANES
    return pl.pallas_call(
        functools.partial(update_kernel, hops, lists_total),
        grid=(lists // CHUNK,),
        out_shape=jax.ShapeDtypeStruct((lists, width), F32),
        in_specs=[
            pl.BlockSpec(before.shape, lambda i: (0, 0, 0)),
            pl.BlockSpec(received.shape, lambda i: (0, 0, 0)),
            pl.BlockSpec((CHUNK, slab), lambda i: (i, 0)),
            pl.BlockSpec((slab, width), lambda i: (0, 0)),
        ],
        out_specs=pl.BlockSpec((CHUNK, width), lambda i: (i, 0)),
        scratch_shapes=[
            pltpu.VMEM((rows, LANES), F32),
            pltpu.VMEM((1, slab), F32),
            pltpu.VMEM((1, slab), F32),
        ],
        compiler_params=params(),
        cost_estimate=pl.CostEstimate(
            flops=2 * lists * width * slab, bytes_accessed=8 * lists * slab, transcendentals=0
        ),
    )(before, received, kt, slab_vectors)


def exchange(copies, axes):
    return lax.all_to_all(copies, axes, 0, 0, tiled=True)


def sum_over_lists(copies):
    partial = jnp.sum(exchange(copies, ("dp", "cx")), axis=0)
    size = lax.axis_size("cz")
    return exchange(jnp.broadcast_to(partial[None], (size,) + partial.shape), "cz")


def body(vectors, centroids):
    dp = lax.axis_size("dp")
    peers = dp * lax.axis_size("cx")
    lists_total = centroids.shape[0] * peers * lax.axis_size("cz")
    hops = tuple(range(dp))
    mine = unit_rows(vectors)
    others = [lax.ppermute(mine, "dp", [((i + hop) % dp, i) for i in range(dp)]) for hop in hops[1:]]
    unit_centroids, own = own_scores(centroids, mine)
    kt, slab_vectors, copies = first_sweep(
        unit_centroids, own, [mine] + others, hops, lists_total, peers
    )
    received = sum_over_lists(copies)
    for sweep in range(1, ITERS):
        before = received
        received = sum_over_lists(next_sweep(before, kt, hops, lists_total, peers))
    partial_numer = update(before, received, kt, slab_vectors, hops, lists_total)
    numerators = lax.psum_scatter(partial_numer, "replica", scatter_dimension=1, tiled=True)
    squares = lax.psum(jnp.sum(numerators * numerators, axis=1), "replica")
    return numerators * lax.rsqrt(squares / VECTOR_WIDTH + 1e-06)[:, None]


def solution(mesh):
    cent = mesh.shape["cent"]
    split = Mesh(
        mesh.devices.reshape(mesh.shape["replica"], mesh.shape["dp"], 4, cent // 4),
        ("replica", "dp", "cx", "cz"),
    )
    placed = (P(("replica", "dp"), None), P(("dp", "cx", "cz"), None))
    return jax.shard_map(
        body, mesh=split, in_specs=placed, out_specs=P(("dp", "cx", "cz"), "replica"), check_vma=False
    )
```

```python
import functools
import math

import jax
import jax.numpy as jnp
from jax import lax
from jax.experimental import pallas as pl
from jax.experimental.pallas import tpu as pltpu
from jax.sharding import Mesh, PartitionSpec as P

VECTOR_WIDTH = 1024
ITERS = 3
SOFTMAX_HEAT = 0.05
EXPONENT = math.log2(math.e) / SOFTMAX_HEAT / VECTOR_WIDTH

LANES = 128
GROUP_ROWS = 8
CHUNK = 256
TILE = 64
KT_PARTS = 4
VMEM_LIMIT = 20 * 1024 * 1024
F32 = jnp.float32
BF16 = jnp.bfloat16

IN_VMEM = pl.BlockSpec(memory_space=pltpu.VMEM)


def params():
    return pltpu.CompilerParams(vmem_limit_bytes=VMEM_LIMIT)


def unit(values):
    scale = lax.rsqrt(jnp.mean(values * values, axis=-1, keepdims=True) + 1e-06)
    return (values * scale).astype(BF16)


def affinity(unit_centroids, unit_vectors):
    scores = lax.dot_general(
        unit_centroids, unit_vectors, (((1,), (1,)), ((), ())), preferred_element_type=F32
    )
    return jnp.exp2(scores * EXPONENT)


def unit_kernel(values_ref, unit_ref):
    unit_ref[...] = unit(values_ref[...])


def unit_rows(values):
    return pl.pallas_call(
        unit_kernel,
        out_shape=jax.ShapeDtypeStruct(values.shape, BF16),
        in_specs=[IN_VMEM],
        out_specs=IN_VMEM,
        compiler_params=params(),
        cost_estimate=pl.CostEstimate(flops=4 * values.size, bytes_accessed=6 * values.size, transcendentals=0),
    )(values)


def own_scores_kernel(centroids_ref, vectors_ref, unit_ref, scores_ref):
    unit_ref[...] = unit(centroids_ref[...])
    scores_ref[...] = affinity(unit_ref[...], vectors_ref[...])


def own_scores(centroids, vectors):
    lists, width = centroids.shape
    block = vectors.shape[0]
    return pl.pallas_call(
        own_scores_kernel,
        grid=(lists // CHUNK,),
        out_shape=(
            jax.ShapeDtypeStruct((lists, width), BF16),
            jax.ShapeDtypeStruct((lists, block), F32),
        ),
        in_specs=[
            pl.BlockSpec((CHUNK, width), lambda i: (i, 0)),
            pl.BlockSpec((block, width), lambda i: (0, 0)),
        ],
        out_specs=(
            pl.BlockSpec((CHUNK, width), lambda i: (i, 0)),
            pl.BlockSpec((CHUNK, block), lambda i: (i, 0)),
        ),
        compiler_params=params(),
        cost_estimate=pl.CostEstimate(
            flops=2 * lists * width * block, bytes_accessed=8 * lists * width, transcendentals=lists * block
        ),
    )(centroids, vectors)


def tile_mass(tile, row_scale, lists_total):
    totals = jnp.sum(tile * row_scale, axis=1, keepdims=True)
    col_scale = (1.0 / lists_total) / totals
    scaled = tile * col_scale
    return jnp.sum(scaled.reshape(-1, GROUP_ROWS, tile.shape[1]), axis=0)


def place_mass(mass, hops, rows_ref, copies_ref):
    row = jnp.sum(mass, axis=0, keepdims=True)
    blocks = len(hops)
    per_block = row.shape[1] // blocks // LANES
    here = lax.axis_index("dp")
    for j, hop in enumerate(hops):
        first = lax.rem(here + hop, blocks) * per_block
        for i in range(per_block):
            at = (j * per_block + i) * LANES
            rows_ref[pl.ds(first + i, 1), :] = row[:, at : at + LANES]
    copies_ref[...] = jnp.broadcast_to(rows_ref[...][None], copies_ref.shape)


def relative_row(rows_ref, hops):
    blocks = len(hops)
    per_block = rows_ref.shape[0] // blocks
    here = lax.axis_index("dp")
    parts = []
    for hop in hops:
        first = lax.rem(here + hop, blocks) * per_block
        parts += [rows_ref[pl.ds(first + i, 1), :] for i in range(per_block)]
    return jnp.concatenate(parts, axis=1)


def first_kernel(hops, lists_total, centroids_ref, own_ref, *refs):
    blocks = len(hops)
    vector_refs = refs[:blocks]
    kt_ref, kt_send_ref, keep_ref, send_ref, copies_ref, slab_ref, mass_ref, rows_ref = refs[blocks:]
    step = pl.program_id(0)
    block = own_ref.shape[1]
    slab = block * blocks

    @pl.when(step == 0)
    def _():
        mass_ref[...] = jnp.zeros_like(mass_ref)
        for j, vector_ref in enumerate(vector_refs):
            slab_ref[pl.ds(j * block, block), :] = vector_ref[...]
        half = keep_ref.shape[1]
        here = lax.axis_index("replica")
        keep_ref[...] = slab_ref[:, pl.ds(pl.multiple_of(here * half, half), half)]
        send_ref[...] = slab_ref[:, pl.ds(pl.multiple_of((1 - here) * half, half), half)]

    kt_ref[:, :block] = own_ref[...]
    kt_ref[:, block:] = affinity(centroids_ref[...], slab_ref[block:, :])
    kt_send_ref[...] = kt_ref[...]
    row_scale = jnp.full((1, slab), 1.0 / slab, F32)
    mass = jnp.zeros(mass_ref.shape, F32)
    for t in range(CHUNK // TILE):
        mass = mass + tile_mass(kt_ref[pl.ds(t * TILE, TILE), :], row_scale, lists_total)
    mass_ref[...] += mass

    @pl.when(step == pl.num_programs(0) - 1)
    def _():
        place_mass(mass_ref[...], hops, rows_ref, copies_ref)


def first_sweep(unit_centroids, own, vectors, hops, lists_total, peers):
    lists, width = unit_centroids.shape
    block = own.shape[1]
    slab = block * len(hops)
    rows = slab // LANES
    whole = lambda shape: pl.BlockSpec(shape, lambda i: (0,) * len(shape))
    return pl.pallas_call(
        functools.partial(first_kernel, hops, lists_total),
        grid=(lists // CHUNK,),
        out_shape=(
            jax.ShapeDtypeStruct((lists, slab), F32),
            pltpu.HBM((lists, slab), F32),
            *[jax.ShapeDtypeStruct((slab, width // 2), BF16)] * 2,
            jax.ShapeDtypeStruct((peers, rows, LANES), F32),
        ),
        in_specs=[
            pl.BlockSpec((CHUNK, width), lambda i: (i, 0)),
            pl.BlockSpec((CHUNK, block), lambda i: (i, 0)),
        ]
        + [whole((block, width))] * len(hops),
        out_specs=(
            *[pl.BlockSpec((CHUNK, slab), lambda i: (i, 0))] * 2,
            *[whole((slab, width // 2))] * 2,
            whole((peers, rows, LANES)),
        ),
        scratch_shapes=[
            pltpu.VMEM((slab, width), BF16),
            pltpu.VMEM((GROUP_ROWS, slab), F32),
            pltpu.VMEM((rows, LANES), F32),
        ],
        compiler_params=params(),
        cost_estimate=pl.CostEstimate(
            flops=2 * lists * width * slab, bytes_accessed=6 * lists * slab, transcendentals=lists * slab
        ),
    )(unit_centroids, own, *vectors)


def row_scale_of(received_ref, rows_ref, hops):
    totals = jnp.sum(received_ref[...], axis=0)
    rows_ref[...] = (1.0 / (totals.shape[0] * totals.shape[1])) / totals
    return relative_row(rows_ref, hops)


def sweep_kernel(hops, lists_total, received_ref, kt_ref, copies_ref, mass_ref, rows_ref, scale_ref):
    step = pl.program_id(0)

    @pl.when(step == 0)
    def _():
        mass_ref[...] = jnp.zeros_like(mass_ref)
        scale_ref[...] = row_scale_of(received_ref, rows_ref, hops)

    row_scale = scale_ref[...]
    mass = jnp.zeros(mass_ref.shape, F32)
    for t in range(CHUNK // TILE):
        mass = mass + tile_mass(kt_ref[pl.ds(t * TILE, TILE), :], row_scale, lists_total)
    mass_ref[...] += mass

    @pl.when(step == pl.num_programs(0) - 1)
    def _():
        place_mass(mass_ref[...], hops, rows_ref, copies_ref)


def next_sweep(received, kt, hops, lists_total, peers):
    lists, slab = kt.shape
    rows = slab // LANES
    return pl.pallas_call(
        functools.partial(sweep_kernel, hops, lists_total),
        grid=(lists // CHUNK,),
        out_shape=jax.ShapeDtypeStruct((peers, rows, LANES), F32),
        in_specs=[
            pl.BlockSpec(received.shape, lambda i: (0, 0, 0)),
            pl.BlockSpec((CHUNK, slab), lambda i: (i, 0)),
        ],
        out_specs=pl.BlockSpec((peers, rows, LANES), lambda i: (0, 0, 0)),
        scratch_shapes=[
            pltpu.VMEM((GROUP_ROWS, slab), F32),
            pltpu.VMEM((rows, LANES), F32),
            pltpu.VMEM((1, slab), F32),
        ],
        compiler_params=params(),
        cost_estimate=pl.CostEstimate(flops=4 * lists * slab, bytes_accessed=4 * lists * slab, transcendentals=0),
    )(received, kt)


def to_row(column):
    return jnp.broadcast_to(column, (LANES, LANES)).T[:1, :]


def to_lanes(row):
    return jnp.broadcast_to(row, (LANES, LANES)).T


def update_kernel(hops, lists_total, before_ref, received_ref, slab_ref, *refs):
    kt_refs, refs = refs[:KT_PARTS], refs[KT_PARTS:]
    *earlier_refs, out_ref, rows_ref, before_scale, scale = refs
    step = pl.program_id(0)

    @pl.when(step == 0)
    def _():
        before_scale[...] = row_scale_of(before_ref, rows_ref, hops)
        scale[...] = row_scale_of(received_ref, rows_ref, hops) * (scale.shape[1] * lists_total)

    kt = jnp.concatenate([kt_ref[...] for kt_ref in kt_refs], axis=0)
    col_scale = (1.0 / lists_total) / jnp.sum(kt * before_scale[...], axis=1, keepdims=True)
    weights = (scale[...] * kt * col_scale).astype(BF16)
    numerators = jnp.dot(weights, slab_ref[...], preferred_element_type=F32)
    if not earlier_refs:
        out_ref[...] = numerators
        return
    earlier_ref, total_ref, squares_ref = earlier_refs[0], earlier_refs[1], out_ref
    total = earlier_ref[...] + numerators
    total_ref[...] = total
    squares = jnp.sum(total * total, axis=1, keepdims=True)
    per_chunk = CHUNK // LANES
    for k in range(per_chunk):
        squares_ref[pl.ds(step * per_chunk + k, 1), :] = to_row(squares[k * LANES : (k + 1) * LANES])


def update(before, received, kt, slab_vectors, hops, lists_total, earlier=None):
    lists, slab = kt.shape
    width = slab_vectors.shape[1]
    rows = slab // LANES
    numerators = jax.ShapeDtypeStruct((lists, width), F32)
    numerators_spec = pl.BlockSpec((CHUNK, width), lambda i: (i, 0))
    squares = jax.ShapeDtypeStruct((lists // LANES, LANES), F32)
    squares_spec = pl.BlockSpec(squares.shape, lambda i: (0, 0))
    first = earlier is None
    return pl.pallas_call(
        functools.partial(update_kernel, hops, lists_total),
        grid=(lists // CHUNK,),
        out_shape=numerators if first else (numerators, squares),
        in_specs=[
            pl.BlockSpec(before.shape, lambda i: (0, 0, 0)),
            pl.BlockSpec(received.shape, lambda i: (0, 0, 0)),
            pl.BlockSpec((slab, width), lambda i: (0, 0)),
        ]
        + [
            pl.BlockSpec((CHUNK // KT_PARTS, slab), lambda i, j=j: (KT_PARTS * i + j, 0))
            for j in range(KT_PARTS)
        ]
        + [numerators_spec] * (not first),
        out_specs=numerators_spec if first else (numerators_spec, squares_spec),
        scratch_shapes=[
            pltpu.VMEM((rows, LANES), F32),
            pltpu.VMEM((1, slab), F32),
            pltpu.VMEM((1, slab), F32),
        ],
        compiler_params=params(),
        cost_estimate=pl.CostEstimate(
            flops=2 * lists * width * slab, bytes_accessed=8 * lists * slab, transcendentals=0
        ),
    )(before, received, slab_vectors, *[kt] * KT_PARTS, *(() if first else (earlier,)))


def finish_kernel(numerators_ref, mine_ref, theirs_ref, out_ref):
    step = pl.program_id(0)
    per_chunk = CHUNK // LANES
    for k in range(per_chunk):
        at = pl.ds(step * per_chunk + k, 1)
        squares = mine_ref[at, :] + theirs_ref[at, :]
        scale = to_lanes(lax.rsqrt(squares / VECTOR_WIDTH + 1e-06))
        lists = pl.ds(k * LANES, LANES)
        for f in range(0, out_ref.shape[1], LANES):
            out_ref[lists, f : f + LANES] = numerators_ref[lists, f : f + LANES] * scale


def finish(numerators, mine, theirs):
    lists, width = numerators.shape
    chunk = pl.BlockSpec((CHUNK, width), lambda i: (i, 0))
    whole = pl.BlockSpec(mine.shape, lambda i: (0, 0))
    return pl.pallas_call(
        finish_kernel,
        grid=(lists // CHUNK,),
        out_shape=jax.ShapeDtypeStruct((lists, width), F32),
        in_specs=[chunk, whole, whole],
        out_specs=chunk,
        compiler_params=params(),
        cost_estimate=pl.CostEstimate(flops=lists * width, bytes_accessed=8 * lists * width, transcendentals=0),
    )(numerators, mine, theirs)


def exchange(copies, axes):
    return lax.all_to_all(copies, axes, 0, 0, tiled=True)


def join_kernel(received_ref, copies_ref):
    copies_ref[...] = jnp.broadcast_to(jnp.sum(received_ref[...], axis=0)[None], copies_ref.shape)


def join(received, peers):
    return pl.pallas_call(
        join_kernel,
        out_shape=jax.ShapeDtypeStruct((peers,) + received.shape[1:], F32),
        in_specs=[IN_VMEM],
        out_specs=IN_VMEM,
        compiler_params=pltpu.CompilerParams(vmem_limit_bytes=1024 * 1024),
    )(received)


def sum_over_lists(copies):
    return exchange(join(exchange(copies, ("dp", "cx")), lax.axis_size("cz")), "cz")


def body(vectors, centroids):
    dp = lax.axis_size("dp")
    peers = dp * lax.axis_size("cx")
    lists_total = centroids.shape[0] * peers * lax.axis_size("cz")
    hops = tuple(range(dp))
    mine = unit_rows(vectors)
    others = [lax.ppermute(mine, "dp", [((i + hop) % dp, i) for i in range(dp)]) for hop in hops[1:]]
    unit_centroids, own = own_scores(centroids, mine)
    kt, kt_sent, kept, sent, copies = first_sweep(
        unit_centroids, own, [mine] + others, hops, lists_total, peers
    )
    swapped = lambda x: lax.ppermute(x, "replica", [(0, 1), (1, 0)])
    other_kt, other_vectors = swapped(kt_sent), swapped(sent)
    received = sum_over_lists(copies)
    for sweep in range(1, ITERS):
        before = received
        received = sum_over_lists(next_sweep(before, kt, hops, lists_total, peers))
    before, received = lax.optimization_barrier((before, received))
    other_before, other_received = swapped(before), swapped(received)
    numerators = update(before, received, kt, kept, hops, lists_total)
    numerators, squares = update(
        other_before, other_received, other_kt, other_vectors, hops, lists_total, numerators
    )
    return finish(numerators, squares, swapped(squares))


def solution(mesh):
    cent = mesh.shape["cent"]
    split = Mesh(
        mesh.devices.reshape(mesh.shape["replica"], mesh.shape["dp"], 4, cent // 4),
        ("replica", "dp", "cx", "cz"),
    )
    placed = (P(("replica", "dp"), None), P(("dp", "cx", "cz"), None))
    return jax.shard_map(
        body, mesh=split, in_specs=placed, out_specs=P(("dp", "cx", "cz"), "replica"), check_vma=False
    )
```

```python
import functools
import math

import jax
import jax.numpy as jnp
from jax import lax
from jax.experimental import pallas as pl
from jax.experimental.pallas import tpu as pltpu
from jax.sharding import Mesh, PartitionSpec as P

VECTOR_WIDTH = 1024
ITERS = 3
SOFTMAX_HEAT = 0.05
EXPONENT = math.log2(math.e) / SOFTMAX_HEAT / VECTOR_WIDTH

LANES = 128
GROUP_ROWS = 8
CHUNK = 256
LONG = 512
TILE = 64
VMEM_LIMIT = 20 * 1024 * 1024
F32 = jnp.float32
BF16 = jnp.bfloat16

IN_VMEM = pl.BlockSpec(memory_space=pltpu.VMEM)


def params():
    return pltpu.CompilerParams(vmem_limit_bytes=VMEM_LIMIT)


def unit(values):
    scale = lax.rsqrt(jnp.mean(values * values, axis=-1, keepdims=True) + 1e-06)
    return (values * scale).astype(BF16)


def affinity(unit_centroids, unit_vectors):
    scores = lax.dot_general(
        unit_centroids, unit_vectors, (((1,), (1,)), ((), ())), preferred_element_type=F32
    )
    return jnp.exp2(scores * EXPONENT)


def share_kernel(values_ref, share_ref, rows_ref, sem):
    rows = share_ref.shape[0]
    first = pl.multiple_of(lax.axis_index("cx") * rows, rows)
    copy = pltpu.make_async_copy(values_ref.at[pl.ds(first, rows), :], rows_ref, sem)
    copy.start()
    copy.wait()
    share_ref[...] = unit(rows_ref[...])


def unit_share(values, shares):
    rows, width = values.shape[0] // shares, values.shape[1]
    return pl.pallas_call(
        share_kernel,
        out_shape=jax.ShapeDtypeStruct((rows, width), BF16),
        in_specs=[pl.BlockSpec(memory_space=pltpu.HBM)],
        out_specs=IN_VMEM,
        scratch_shapes=[pltpu.VMEM((rows, width), F32), pltpu.SemaphoreType.DMA(())],
        compiler_params=params(),
        cost_estimate=pl.CostEstimate(flops=4 * rows * width, bytes_accessed=6 * rows * width, transcendentals=0),
    )(pltpu.with_memory_space_constraint(values, pltpu.HBM))


def unit_kernel(values_ref, share_ref, unit_ref):
    unit_ref[...] = unit(values_ref[...])


def unit_rows(values, share):
    return pl.pallas_call(
        unit_kernel,
        out_shape=jax.ShapeDtypeStruct(values.shape, BF16),
        in_specs=[IN_VMEM, pl.BlockSpec(memory_space=pl.ANY)],
        out_specs=IN_VMEM,
        compiler_params=params(),
        cost_estimate=pl.CostEstimate(flops=4 * values.size, bytes_accessed=6 * values.size, transcendentals=0),
    )(values, share)


def own_scores_kernel(centroids_ref, vectors_ref, unit_ref, scores_ref):
    unit_ref[...] = unit(centroids_ref[...])
    scores_ref[...] = affinity(unit_ref[...], vectors_ref[...])


def own_scores(centroids, vectors):
    lists, width = centroids.shape
    block = vectors.shape[0]
    return pl.pallas_call(
        own_scores_kernel,
        grid=(lists // CHUNK,),
        out_shape=(
            jax.ShapeDtypeStruct((lists, width), BF16),
            jax.ShapeDtypeStruct((lists, block), F32),
        ),
        in_specs=[
            pl.BlockSpec((CHUNK, width), lambda i: (i, 0)),
            pl.BlockSpec((block, width), lambda i: (0, 0)),
        ],
        out_specs=(
            pl.BlockSpec((CHUNK, width), lambda i: (i, 0)),
            pl.BlockSpec((CHUNK, block), lambda i: (i, 0)),
        ),
        compiler_params=params(),
        cost_estimate=pl.CostEstimate(
            flops=2 * lists * width * block, bytes_accessed=8 * lists * width, transcendentals=lists * block
        ),
    )(centroids, vectors)


def scaled_lists(kt, row_scale, lists_total):
    totals = jnp.sum(kt * row_scale, axis=1, keepdims=True)
    return kt * ((1.0 / lists_total) / totals)


def place_mass(mass, hops, rows_ref, copies_ref):
    row = jnp.sum(mass, axis=0, keepdims=True)
    blocks = len(hops)
    per_block = row.shape[1] // blocks // LANES
    here = lax.axis_index("dp")
    for j, hop in enumerate(hops):
        first = lax.rem(here + hop, blocks) * per_block
        for i in range(per_block):
            at = (j * per_block + i) * LANES
            rows_ref[pl.ds(first + i, 1), :] = row[:, at : at + LANES]
    copies_ref[...] = jnp.broadcast_to(rows_ref[...][None], copies_ref.shape)


def relative_row(rows_ref, hops):
    blocks = len(hops)
    per_block = rows_ref.shape[0] // blocks
    here = lax.axis_index("dp")
    parts = []
    for hop in hops:
        first = lax.rem(here + hop, blocks) * per_block
        parts += [rows_ref[pl.ds(first + i, 1), :] for i in range(per_block)]
    return jnp.concatenate(parts, axis=1)


def sweep_lists(kt_ref, row_scale, lists, lists_total, scaled_ref=None):
    mass = jnp.zeros((GROUP_ROWS, kt_ref.shape[1]), F32)
    for t in range(lists.start, lists.stop, TILE):
        scaled = scaled_lists(kt_ref[pl.ds(t, TILE), :], row_scale, lists_total)
        mass = mass + jnp.sum(scaled.reshape(-1, GROUP_ROWS, scaled.shape[1]), axis=0)
        if scaled_ref is not None:
            scaled_ref[pl.ds(t, TILE), :] = scaled
    return mass


def chunks_of(lists, size=CHUNK):
    return [range(at, at + size) for at in range(0, lists, size)]


def near_kernel(centroids_ref, *refs):
    *vector_refs, scores_ref = refs
    block = vector_refs[0].shape[0]
    for chunk in chunks_of(scores_ref.shape[0], LONG):
        rows = pl.ds(chunk.start, LONG)
        for j, vector_ref in enumerate(vector_refs):
            scores_ref[rows, j * block : (j + 1) * block] = affinity(centroids_ref[rows, :], vector_ref[...])


def near_scores(unit_centroids, vectors):
    lists, width = unit_centroids.shape
    columns = sum(v.shape[0] for v in vectors)
    return pl.pallas_call(
        near_kernel,
        out_shape=jax.ShapeDtypeStruct((lists, columns), F32),
        in_specs=[IN_VMEM] * (1 + len(vectors)),
        out_specs=IN_VMEM,
        compiler_params=params(),
        cost_estimate=pl.CostEstimate(
            flops=2 * lists * width * columns, bytes_accessed=4 * lists * width, transcendentals=lists * columns
        ),
    )(unit_centroids, *vectors)


def first_kernel(hops, lists_total, blocks, centroids_ref, own_ref, near_ref, *refs):
    vector_refs = refs[:blocks]
    kt_ref, kt_send_ref, keep_ref, send_ref, copies_ref, slab_ref, rows_ref, sems = refs[blocks:]
    lists, slab = kt_ref.shape
    block = own_ref.shape[1]
    known = block + near_ref.shape[1]
    for j, vector_ref in enumerate(vector_refs[: len(hops) - 1]):
        slab_ref[pl.ds(j * block, block), :] = vector_ref[...]
    shares = vector_refs[len(hops) - 1 :]
    for j, share_ref in enumerate(shares):
        rows = share_ref.shape[0]
        at = lax.rem(lax.axis_index("cx") + j, len(shares)) * rows
        slab_ref[pl.ds(pl.multiple_of(known + at, rows), rows), :] = share_ref[...]
    half = keep_ref.shape[1]
    here = lax.axis_index("replica")
    keep_ref[...] = slab_ref[:, pl.ds(pl.multiple_of(here * half, half), half)]
    send_ref[...] = slab_ref[:, pl.ds(pl.multiple_of((1 - here) * half, half), half)]
    row_scale = jnp.full((1, slab), 1.0 / slab, F32)
    mass = jnp.zeros((GROUP_ROWS, slab), F32)
    sends = []
    for c, chunk in enumerate(chunks_of(lists, LONG)):
        rows = pl.ds(chunk.start, LONG)
        kt_ref[rows, :block] = own_ref[rows, :]
        kt_ref[rows, block:known] = near_ref[rows, :]
        kt_ref[rows, known:] = affinity(centroids_ref[rows, :], slab_ref[known:, :])
        sends.append(pltpu.make_async_copy(kt_ref.at[rows, :], kt_send_ref.at[rows, :], sems.at[c]))
        sends[-1].start()
        mass = mass + sweep_lists(kt_ref, row_scale, chunk, lists_total)
    place_mass(mass, hops, rows_ref, copies_ref)
    for send in sends:
        send.wait()


def first_sweep(unit_centroids, own, near, vectors, hops, lists_total, peers):
    lists, width = unit_centroids.shape
    slab = own.shape[1] * len(hops)
    rows = slab // LANES
    return pl.pallas_call(
        functools.partial(first_kernel, hops, lists_total, len(vectors)),
        out_shape=(
            jax.ShapeDtypeStruct((lists, slab), F32),
            pltpu.HBM((lists, slab), F32),
            *[jax.ShapeDtypeStruct((slab, width // 2), BF16)] * 2,
            jax.ShapeDtypeStruct((peers, rows, LANES), F32),
        ),
        in_specs=[IN_VMEM] * (3 + len(vectors)),
        out_specs=(IN_VMEM, pl.BlockSpec(memory_space=pltpu.HBM), IN_VMEM, IN_VMEM, IN_VMEM),
        scratch_shapes=[
            pltpu.VMEM((slab, width), BF16),
            pltpu.VMEM((rows, LANES), F32),
            pltpu.SemaphoreType.DMA((lists // LONG,)),
        ],
        compiler_params=params(),
        cost_estimate=pl.CostEstimate(
            flops=lists * width * slab // 2, bytes_accessed=6 * lists * slab, transcendentals=lists * slab // 4
        ),
    )(unit_centroids, own, near, *vectors)


def row_scale_of(received_ref, rows_ref, hops):
    totals = jnp.sum(received_ref[...], axis=0)
    rows_ref[...] = (1.0 / (totals.shape[0] * totals.shape[1])) / totals
    return relative_row(rows_ref, hops)


def sweep_kernel(hops, lists_total, received_ref, kt_ref, copies_ref, *refs):
    *scaled_refs, rows_ref = refs
    row_scale = row_scale_of(received_ref, rows_ref, hops)
    mass = sweep_lists(kt_ref, row_scale, range(kt_ref.shape[0]), lists_total, *scaled_refs)
    place_mass(mass, hops, rows_ref, copies_ref)


def next_sweep(received, kt, hops, lists_total, peers, last):
    lists, slab = kt.shape
    rows = slab // LANES
    outs = [jax.ShapeDtypeStruct((peers, rows, LANES), F32)] + [jax.ShapeDtypeStruct((lists, slab), F32)] * last
    return pl.pallas_call(
        functools.partial(sweep_kernel, hops, lists_total),
        out_shape=outs,
        in_specs=[IN_VMEM] * 2,
        out_specs=[IN_VMEM] * len(outs),
        scratch_shapes=[pltpu.VMEM((rows, LANES), F32)],
        compiler_params=params(),
        cost_estimate=pl.CostEstimate(flops=4 * lists * slab, bytes_accessed=4 * lists * slab, transcendentals=0),
    )(received, kt)


def to_row(column):
    return jnp.broadcast_to(column, (LANES, LANES)).T[:1, :]


def to_lanes(row):
    return jnp.broadcast_to(row, (LANES, LANES)).T


def own_update_kernel(hops, lists_total, received_ref, scaled_ref, slab_ref, out_ref, weights_ref, rows_ref):
    lists, slab = scaled_ref.shape
    scale = row_scale_of(received_ref, rows_ref, hops) * (slab * lists_total)
    for chunk in chunks_of(lists, LONG):
        rows = pl.ds(chunk.start, LONG)
        for t in range(chunk.start, chunk.stop, TILE):
            weights_ref[pl.ds(t, TILE), :] = (scaled_ref[pl.ds(t, TILE), :] * scale).astype(BF16)
        out_ref[rows, :] = jnp.dot(weights_ref[rows, :], slab_ref[...], preferred_element_type=F32)


def own_update(received, scaled, slab_vectors, hops, lists_total):
    lists, slab = scaled.shape
    width = slab_vectors.shape[1]
    return pl.pallas_call(
        functools.partial(own_update_kernel, hops, lists_total),
        out_shape=jax.ShapeDtypeStruct((lists, width), F32),
        in_specs=[IN_VMEM] * 3,
        out_specs=IN_VMEM,
        scratch_shapes=[pltpu.VMEM((lists, slab), BF16), pltpu.VMEM((slab // LANES, LANES), F32)],
        compiler_params=params(),
        cost_estimate=pl.CostEstimate(
            flops=2 * lists * width * slab, bytes_accessed=6 * lists * slab, transcendentals=0
        ),
    )(received, scaled, slab_vectors)


def other_update_kernel(
    hops, lists_total, before_ref, received_ref, slab_ref, earlier_ref, kt_ref,
    total_ref, squares_ref, incoming_ref, weights_ref, rows_ref, sems,
):
    lists, slab = kt_ref.shape
    copies = []
    for c, chunk in enumerate(chunks_of(lists)):
        rows = pl.ds(chunk.start, CHUNK)
        copies.append(pltpu.make_async_copy(kt_ref.at[rows, :], incoming_ref.at[rows, :], sems.at[c]))
        copies[-1].start()
    before_scale = row_scale_of(before_ref, rows_ref, hops)
    scale = row_scale_of(received_ref, rows_ref, hops) * (slab * lists_total)
    for chunk in chunks_of(lists, LONG):
        rows = pl.ds(chunk.start, LONG)
        for t in range(chunk.start, chunk.stop, TILE):
            if t % CHUNK == 0:
                copies[t // CHUNK].wait()
            scaled = scaled_lists(incoming_ref[pl.ds(t, TILE), :], before_scale, lists_total)
            weights_ref[pl.ds(t, TILE), :] = (scaled * scale).astype(BF16)
        total = jnp.dot(weights_ref[rows, :], slab_ref[...], preferred_element_type=F32)
        total = total + earlier_ref[rows, :]
        total_ref[rows, :] = total
        squares = jnp.sum(total * total, axis=1, keepdims=True)
        for k in range(LONG // LANES):
            at = chunk.start // LANES + k
            squares_ref[at : at + 1, :] = to_row(squares[k * LANES : (k + 1) * LANES])


def other_update(before, received, slab_vectors, earlier, kt, hops, lists_total):
    lists, slab = kt.shape
    width = slab_vectors.shape[1]
    return pl.pallas_call(
        functools.partial(other_update_kernel, hops, lists_total),
        out_shape=(
            jax.ShapeDtypeStruct((lists, width), F32),
            jax.ShapeDtypeStruct((lists // LANES, LANES), F32),
        ),
        in_specs=[IN_VMEM] * 4 + [pl.BlockSpec(memory_space=pltpu.HBM)],
        out_specs=(IN_VMEM, IN_VMEM),
        scratch_shapes=[
            pltpu.VMEM((lists, slab), F32),
            pltpu.VMEM((lists, slab), BF16),
            pltpu.VMEM((slab // LANES, LANES), F32),
            pltpu.SemaphoreType.DMA((lists // CHUNK,)),
        ],
        compiler_params=params(),
        cost_estimate=pl.CostEstimate(
            flops=2 * lists * width * slab, bytes_accessed=8 * lists * slab, transcendentals=0
        ),
    )(before, received, slab_vectors, earlier, kt)


def finish_kernel(numerators_ref, mine_ref, theirs_ref, out_ref, scaled_ref, sems):
    lists, width = numerators_ref.shape
    scales = lax.rsqrt((mine_ref[...] + theirs_ref[...]) / VECTOR_WIDTH + 1e-06)
    copies = []
    for c, chunk in enumerate(chunks_of(lists)):
        for k in range(CHUNK // LANES):
            at = chunk.start + k * LANES
            scale = to_lanes(scales[at // LANES : at // LANES + 1, :])
            for f in range(0, width, LANES):
                scaled_ref[at : at + LANES, f : f + LANES] = numerators_ref[at : at + LANES, f : f + LANES] * scale
        rows = pl.ds(chunk.start, CHUNK)
        copies.append(pltpu.make_async_copy(scaled_ref.at[rows, :], out_ref.at[rows, :], sems.at[c]))
        copies[-1].start()
    for copy in copies:
        copy.wait()


def finish(numerators, mine, theirs):
    lists, width = numerators.shape
    return pl.pallas_call(
        finish_kernel,
        out_shape=jax.ShapeDtypeStruct((lists, width), F32),
        in_specs=[IN_VMEM] * 3,
        out_specs=pl.BlockSpec(memory_space=pltpu.HBM),
        scratch_shapes=[
            pltpu.VMEM((lists, width), F32),
            pltpu.SemaphoreType.DMA((lists // CHUNK,)),
        ],
        compiler_params=params(),
        cost_estimate=pl.CostEstimate(flops=lists * width, bytes_accessed=8 * lists * width, transcendentals=0),
    )(numerators, mine, theirs)


def exchange(copies, axes):
    return lax.all_to_all(copies, axes, 0, 0, tiled=True)


def join_kernel(received_ref, copies_ref):
    copies_ref[...] = jnp.broadcast_to(jnp.sum(received_ref[...], axis=0)[None], copies_ref.shape)


def join(received, peers):
    return pl.pallas_call(
        join_kernel,
        out_shape=jax.ShapeDtypeStruct((peers,) + received.shape[1:], F32),
        in_specs=[IN_VMEM],
        out_specs=IN_VMEM,
        compiler_params=pltpu.CompilerParams(vmem_limit_bytes=1024 * 1024),
    )(received)


def sum_over_lists(copies):
    return exchange(join(exchange(copies, ("dp", "cx")), lax.axis_size("cz")), "cz")


def body(vectors, centroids):
    dp = lax.axis_size("dp")
    peers = dp * lax.axis_size("cx")
    lists_total = centroids.shape[0] * peers * lax.axis_size("cz")
    hops = (0, 1, dp - 1, 2)
    cx = lax.axis_size("cx")
    share = unit_share(vectors, cx)
    mine = unit_rows(vectors, share)
    from_hop = lambda x, axis, hop, size: lax.ppermute(x, axis, [((i + hop) % size, i) for i in range(size)])
    far = from_hop(share, "dp", hops[3], dp)
    far, ready = lax.optimization_barrier((far, mine))
    near = [from_hop(ready, "dp", hop, dp) for hop in hops[1:3]]
    far = [far] + [from_hop(far, "cx", hop, cx) for hop in range(1, cx)]
    unit_centroids, own = own_scores(centroids, mine)
    near_kt = near_scores(unit_centroids, near)
    kt, kt_sent, kept, sent, copies = first_sweep(
        unit_centroids, own, near_kt, [mine, *near, *far], hops, lists_total, peers
    )
    swapped = lambda x: lax.ppermute(x, "replica", [(0, 1), (1, 0)])
    other_kt, other_vectors = swapped(kt_sent), swapped(sent)
    received = sum_over_lists(copies)
    for sweep in range(1, ITERS):
        before = received
        copies, *scaled = next_sweep(before, kt, hops, lists_total, peers, sweep == ITERS - 1)
        received = sum_over_lists(copies)
    before, received = lax.optimization_barrier((before, received))
    other_before, other_received = swapped(before), swapped(received)
    own_numerators = own_update(received, scaled[0], kept, hops, lists_total)
    numerators, squares = other_update(
        other_before, other_received, other_vectors, own_numerators, other_kt, hops, lists_total
    )
    return finish(numerators, squares, swapped(squares))


def solution(mesh):
    cent = mesh.shape["cent"]
    split = Mesh(
        mesh.devices.reshape(mesh.shape["replica"], mesh.shape["dp"], 4, cent // 4),
        ("replica", "dp", "cx", "cz"),
    )
    placed = (P(("replica", "dp"), None), P(("dp", "cx", "cz"), None))
    return jax.shard_map(
        body, mesh=split, in_specs=placed, out_specs=P(("dp", "cx", "cz"), "replica"), check_vma=False
    )
```

```python
import functools
import math

import jax
import jax.numpy as jnp
from jax import lax
from jax.experimental import pallas as pl
from jax.experimental.pallas import tpu as pltpu
from jax.sharding import Mesh, PartitionSpec as P

VECTOR_WIDTH = 1024
ITERS = 3
SOFTMAX_HEAT = 0.05
EXPONENT = math.log2(math.e) / SOFTMAX_HEAT / VECTOR_WIDTH

LANES = 128
GROUP_ROWS = 8
CHUNK = 256
LONG = 512
TILE = 64
VMEM_LIMIT = 20 * 1024 * 1024
F32 = jnp.float32
BF16 = jnp.bfloat16

IN_VMEM = pl.BlockSpec(memory_space=pltpu.VMEM)


def params():
    return pltpu.CompilerParams(vmem_limit_bytes=VMEM_LIMIT)


def unit(values):
    scale = lax.rsqrt(jnp.mean(values * values, axis=-1, keepdims=True) + 1e-06)
    return (values * scale).astype(BF16)


def affinity(unit_centroids, unit_vectors):
    scores = lax.dot_general(
        unit_centroids, unit_vectors, (((1,), (1,)), ((), ())), preferred_element_type=F32
    )
    return jnp.exp2(scores * EXPONENT)


def share_kernel(values_ref, share_ref, rows_ref, sem):
    rows = share_ref.shape[0]
    first = pl.multiple_of(lax.axis_index("cx") * rows, rows)
    copy = pltpu.make_async_copy(values_ref.at[pl.ds(first, rows), :], rows_ref, sem)
    copy.start()
    copy.wait()
    share_ref[...] = unit(rows_ref[...])


def unit_share(values, shares):
    rows, width = values.shape[0] // shares, values.shape[1]
    return pl.pallas_call(
        share_kernel,
        out_shape=jax.ShapeDtypeStruct((rows, width), BF16),
        in_specs=[pl.BlockSpec(memory_space=pltpu.HBM)],
        out_specs=IN_VMEM,
        scratch_shapes=[pltpu.VMEM((rows, width), F32), pltpu.SemaphoreType.DMA(())],
        compiler_params=params(),
        cost_estimate=pl.CostEstimate(flops=4 * rows * width, bytes_accessed=6 * rows * width, transcendentals=0),
    )(pltpu.with_memory_space_constraint(values, pltpu.HBM))


def unit_kernel(values_ref, share_ref, unit_ref):
    unit_ref[...] = unit(values_ref[...])


def unit_rows(values, share):
    return pl.pallas_call(
        unit_kernel,
        out_shape=jax.ShapeDtypeStruct(values.shape, BF16),
        in_specs=[IN_VMEM, pl.BlockSpec(memory_space=pl.ANY)],
        out_specs=IN_VMEM,
        compiler_params=params(),
        cost_estimate=pl.CostEstimate(flops=4 * values.size, bytes_accessed=6 * values.size, transcendentals=0),
    )(values, share)


def stream_in(source_ref, held_ref, sems):
    copies = []
    for c, chunk in enumerate(chunks_of(source_ref.shape[0])):
        rows = pl.ds(chunk.start, CHUNK)
        copies.append(pltpu.make_async_copy(source_ref.at[rows, :], held_ref.at[rows, :], sems.at[c]))
        copies[-1].start()
    return copies


def centroids_kernel(centroids_ref, unit_ref, held_ref, sems):
    copies = stream_in(centroids_ref, held_ref, sems)
    for c, chunk in enumerate(chunks_of(centroids_ref.shape[0])):
        copies[c].wait()
        for t in range(chunk.start, chunk.stop, TILE):
            unit_ref[pl.ds(t, TILE), :] = unit(held_ref[pl.ds(t, TILE), :])


def unit_lists(centroids):
    lists, width = centroids.shape
    return pl.pallas_call(
        centroids_kernel,
        out_shape=jax.ShapeDtypeStruct((lists, width), BF16),
        in_specs=[pl.BlockSpec(memory_space=pltpu.HBM)],
        out_specs=IN_VMEM,
        scratch_shapes=[pltpu.VMEM((lists, width), F32), pltpu.SemaphoreType.DMA((lists // CHUNK,))],
        compiler_params=params(),
        cost_estimate=pl.CostEstimate(flops=4 * lists * width, bytes_accessed=6 * lists * width, transcendentals=0),
    )(pltpu.with_memory_space_constraint(centroids, pltpu.HBM))


def scaled_lists(kt, row_scale, lists_total):
    totals = jnp.sum(kt * row_scale, axis=1, keepdims=True)
    return kt * ((1.0 / lists_total) / totals)


def place_mass(mass, hops, rows_ref, copies_ref):
    row = jnp.sum(mass, axis=0, keepdims=True)
    blocks = len(hops)
    per_block = row.shape[1] // blocks // LANES
    here = lax.axis_index("dp")
    for j, hop in enumerate(hops):
        first = lax.rem(here + hop, blocks) * per_block
        for i in range(per_block):
            at = (j * per_block + i) * LANES
            rows_ref[pl.ds(first + i, 1), :] = row[:, at : at + LANES]
    copies_ref[...] = jnp.broadcast_to(rows_ref[...][None], copies_ref.shape)


def relative_row(rows_ref, hops):
    blocks = len(hops)
    per_block = rows_ref.shape[0] // blocks
    here = lax.axis_index("dp")
    parts = []
    for hop in hops:
        first = lax.rem(here + hop, blocks) * per_block
        parts += [rows_ref[pl.ds(first + i, 1), :] for i in range(per_block)]
    return jnp.concatenate(parts, axis=1)


def sweep_lists(kt_ref, row_scale, lists, lists_total, scaled_ref=None):
    mass = jnp.zeros((GROUP_ROWS, kt_ref.shape[1]), F32)
    for t in range(lists.start, lists.stop, TILE):
        scaled = scaled_lists(kt_ref[pl.ds(t, TILE), :], row_scale, lists_total)
        mass = mass + jnp.sum(scaled.reshape(-1, GROUP_ROWS, scaled.shape[1]), axis=0)
        if scaled_ref is not None:
            scaled_ref[pl.ds(t, TILE), :] = scaled
    return mass


def chunks_of(lists, size=CHUNK):
    return [range(at, at + size) for at in range(0, lists, size)]


def score_lists(centroids_ref, vectors_ref, scores_ref):
    for chunk in chunks_of(scores_ref.shape[0], LONG):
        rows = pl.ds(chunk.start, LONG)
        scores_ref[rows, :] = affinity(centroids_ref[rows, :], vectors_ref[...])


def far_kernel(centroids_ref, *refs):
    *share_refs, vectors_ref, scores_ref = refs
    for j, share_ref in enumerate(share_refs):
        rows = share_ref.shape[0]
        at = lax.rem(lax.axis_index("cx") + j, len(share_refs)) * rows
        vectors_ref[pl.ds(pl.multiple_of(at, rows), rows), :] = share_ref[...]
    score_lists(centroids_ref, vectors_ref, scores_ref)


def score_cost(lists, width, columns):
    return pl.CostEstimate(
        flops=2 * lists * width * columns, bytes_accessed=4 * lists * width, transcendentals=lists * columns
    )


def block_scores(unit_centroids, vectors):
    lists, width = unit_centroids.shape
    block = vectors.shape[0]
    return pl.pallas_call(
        score_lists,
        out_shape=jax.ShapeDtypeStruct((lists, block), F32),
        in_specs=[IN_VMEM] * 2,
        out_specs=IN_VMEM,
        compiler_params=params(),
        cost_estimate=score_cost(lists, width, block),
    )(unit_centroids, vectors)


def far_scores(unit_centroids, shares):
    lists, width = unit_centroids.shape
    block = shares[0].shape[0] * len(shares)
    return pl.pallas_call(
        far_kernel,
        out_shape=(jax.ShapeDtypeStruct((block, width), BF16), jax.ShapeDtypeStruct((lists, block), F32)),
        in_specs=[IN_VMEM] * (1 + len(shares)),
        out_specs=(IN_VMEM, IN_VMEM),
        compiler_params=params(),
        cost_estimate=score_cost(lists, width, block),
    )(unit_centroids, *shares)


def first_kernel(hops, lists_total, centroids_ref, own_ref, far_ref, *refs):
    blocks = len(hops)
    vector_refs = refs[:blocks]
    kt_ref, kt_send_ref, keep_ref, send_ref, copies_ref, slab_ref, rows_ref, sems = refs[blocks:]
    lists, slab = kt_ref.shape
    block = own_ref.shape[1]
    known = block + far_ref.shape[1]
    for j, vector_ref in enumerate(vector_refs):
        slab_ref[pl.ds(j * block, block), :] = vector_ref[...]
    half = keep_ref.shape[1]
    here = lax.axis_index("replica")
    keep_ref[...] = slab_ref[:, pl.ds(pl.multiple_of(here * half, half), half)]
    send_ref[...] = slab_ref[:, pl.ds(pl.multiple_of((1 - here) * half, half), half)]
    row_scale = jnp.full((1, slab), 1.0 / slab, F32)
    mass = jnp.zeros((GROUP_ROWS, slab), F32)
    sends = []
    for c, chunk in enumerate(chunks_of(lists, LONG)):
        rows = pl.ds(chunk.start, LONG)
        kt_ref[rows, :block] = own_ref[rows, :]
        kt_ref[rows, block:known] = far_ref[rows, :]
        kt_ref[rows, known:] = affinity(centroids_ref[rows, :], slab_ref[known:, :])
        sends.append(pltpu.make_async_copy(kt_ref.at[rows, :], kt_send_ref.at[rows, :], sems.at[c]))
        sends[-1].start()
        mass = mass + sweep_lists(kt_ref, row_scale, chunk, lists_total)
    place_mass(mass, hops, rows_ref, copies_ref)
    for send in sends:
        send.wait()


def first_sweep(unit_centroids, own, far, vectors, hops, lists_total, peers):
    lists, width = unit_centroids.shape
    slab = own.shape[1] * len(hops)
    rows = slab // LANES
    return pl.pallas_call(
        functools.partial(first_kernel, hops, lists_total),
        out_shape=(
            jax.ShapeDtypeStruct((lists, slab), F32),
            pltpu.HBM((lists, slab), F32),
            *[jax.ShapeDtypeStruct((slab, width // 2), BF16)] * 2,
            jax.ShapeDtypeStruct((peers, rows, LANES), F32),
        ),
        in_specs=[IN_VMEM] * (3 + len(vectors)),
        out_specs=(IN_VMEM, pl.BlockSpec(memory_space=pltpu.HBM), IN_VMEM, IN_VMEM, IN_VMEM),
        scratch_shapes=[
            pltpu.VMEM((slab, width), BF16),
            pltpu.VMEM((rows, LANES), F32),
            pltpu.SemaphoreType.DMA((lists // LONG,)),
        ],
        compiler_params=params(),
        cost_estimate=pl.CostEstimate(
            flops=lists * width * slab, bytes_accessed=6 * lists * slab, transcendentals=lists * slab // 2
        ),
    )(unit_centroids, own, far, *vectors)


def row_scale_of(received_ref, rows_ref, hops):
    totals = jnp.sum(received_ref[...], axis=0)
    rows_ref[...] = (1.0 / (totals.shape[0] * totals.shape[1])) / totals
    return relative_row(rows_ref, hops)


def sweep_kernel(hops, lists_total, received_ref, kt_ref, copies_ref, *refs):
    *scaled_refs, rows_ref = refs
    row_scale = row_scale_of(received_ref, rows_ref, hops)
    mass = sweep_lists(kt_ref, row_scale, range(kt_ref.shape[0]), lists_total, *scaled_refs)
    place_mass(mass, hops, rows_ref, copies_ref)


def next_sweep(received, kt, hops, lists_total, peers, last):
    lists, slab = kt.shape
    rows = slab // LANES
    outs = [jax.ShapeDtypeStruct((peers, rows, LANES), F32)] + [jax.ShapeDtypeStruct((lists, slab), F32)] * last
    return pl.pallas_call(
        functools.partial(sweep_kernel, hops, lists_total),
        out_shape=outs,
        in_specs=[IN_VMEM] * 2,
        out_specs=[IN_VMEM] * len(outs),
        scratch_shapes=[pltpu.VMEM((rows, LANES), F32)],
        compiler_params=params(),
        cost_estimate=pl.CostEstimate(flops=4 * lists * slab, bytes_accessed=4 * lists * slab, transcendentals=0),
    )(received, kt)


def to_row(column):
    return jnp.broadcast_to(column, (LANES, LANES)).T[:1, :]


def to_lanes(row):
    return jnp.broadcast_to(row, (LANES, LANES)).T


def write_weights(scaled_ref, scale, weights_ref, lists):
    for t in range(lists.start, lists.stop, TILE):
        weights_ref[pl.ds(t, TILE), :] = (scaled_ref[pl.ds(t, TILE), :] * scale).astype(BF16)


def own_update_kernel(
    hops, lists_total, received_ref, scaled_ref, slab_ref, other_before_ref, other_kt_ref,
    out_ref, other_scaled_ref, weights_ref, rows_ref, sems,
):
    lists, slab = scaled_ref.shape
    copies = stream_in(other_kt_ref, other_scaled_ref, sems)
    scale = row_scale_of(received_ref, rows_ref, hops) * (slab * lists_total)
    other_before_scale = row_scale_of(other_before_ref, rows_ref, hops)
    for chunk in chunks_of(lists, LONG):
        rows = pl.ds(chunk.start, LONG)
        write_weights(scaled_ref, scale, weights_ref, chunk)
        out_ref[rows, :] = jnp.dot(weights_ref[rows, :], slab_ref[...], preferred_element_type=F32)
    for c, chunk in enumerate(chunks_of(lists)):
        copies[c].wait()
        for t in range(chunk.start, chunk.stop, TILE):
            rows = pl.ds(t, TILE)
            other_scaled_ref[rows, :] = scaled_lists(other_scaled_ref[rows, :], other_before_scale, lists_total)


def own_update(received, scaled, slab_vectors, other_before, other_kt, hops, lists_total):
    lists, slab = scaled.shape
    width = slab_vectors.shape[1]
    return pl.pallas_call(
        functools.partial(own_update_kernel, hops, lists_total),
        out_shape=(jax.ShapeDtypeStruct((lists, width), F32), jax.ShapeDtypeStruct((lists, slab), F32)),
        in_specs=[IN_VMEM] * 4 + [pl.BlockSpec(memory_space=pltpu.HBM)],
        out_specs=(IN_VMEM, IN_VMEM),
        scratch_shapes=[
            pltpu.VMEM((lists, slab), BF16),
            pltpu.VMEM((slab // LANES, LANES), F32),
            pltpu.SemaphoreType.DMA((lists // CHUNK,)),
        ],
        compiler_params=params(),
        cost_estimate=pl.CostEstimate(
            flops=2 * lists * width * slab, bytes_accessed=6 * lists * slab, transcendentals=0
        ),
    )(received, scaled, slab_vectors, other_before, other_kt)


def other_update_kernel(
    hops, lists_total, received_ref, scaled_ref, slab_ref, earlier_ref,
    total_ref, squares_ref, weights_ref, rows_ref,
):
    lists, slab = scaled_ref.shape
    scale = row_scale_of(received_ref, rows_ref, hops) * (slab * lists_total)
    for chunk in chunks_of(lists, LONG):
        rows = pl.ds(chunk.start, LONG)
        write_weights(scaled_ref, scale, weights_ref, chunk)
        total = jnp.dot(weights_ref[rows, :], slab_ref[...], preferred_element_type=F32)
        total = total + earlier_ref[rows, :]
        total_ref[rows, :] = total
        squares = jnp.sum(total * total, axis=1, keepdims=True)
        for k in range(LONG // LANES):
            at = chunk.start // LANES + k
            squares_ref[at : at + 1, :] = to_row(squares[k * LANES : (k + 1) * LANES])


def other_update(received, scaled, slab_vectors, earlier, hops, lists_total):
    lists, slab = scaled.shape
    width = slab_vectors.shape[1]
    return pl.pallas_call(
        functools.partial(other_update_kernel, hops, lists_total),
        out_shape=(
            jax.ShapeDtypeStruct((lists, width), F32),
            jax.ShapeDtypeStruct((lists // LANES, LANES), F32),
        ),
        in_specs=[IN_VMEM] * 4,
        out_specs=(IN_VMEM, IN_VMEM),
        scratch_shapes=[pltpu.VMEM((lists, slab), BF16), pltpu.VMEM((slab // LANES, LANES), F32)],
        compiler_params=params(),
        cost_estimate=pl.CostEstimate(
            flops=2 * lists * width * slab, bytes_accessed=8 * lists * slab, transcendentals=0
        ),
    )(received, scaled, slab_vectors, earlier)


def finish_kernel(numerators_ref, mine_ref, theirs_ref, out_ref, scaled_ref, sems):
    lists, width = numerators_ref.shape
    scales = lax.rsqrt((mine_ref[...] + theirs_ref[...]) / VECTOR_WIDTH + 1e-06)
    copies = []
    for c, chunk in enumerate(chunks_of(lists)):
        for k in range(CHUNK // LANES):
            at = chunk.start + k * LANES
            scale = to_lanes(scales[at // LANES : at // LANES + 1, :])
            for f in range(0, width, LANES):
                scaled_ref[at : at + LANES, f : f + LANES] = numerators_ref[at : at + LANES, f : f + LANES] * scale
        rows = pl.ds(chunk.start, CHUNK)
        copies.append(pltpu.make_async_copy(scaled_ref.at[rows, :], out_ref.at[rows, :], sems.at[c]))
        copies[-1].start()
    for copy in copies:
        copy.wait()


def finish(numerators, mine, theirs):
    lists, width = numerators.shape
    return pl.pallas_call(
        finish_kernel,
        out_shape=jax.ShapeDtypeStruct((lists, width), F32),
        in_specs=[IN_VMEM] * 3,
        out_specs=pl.BlockSpec(memory_space=pltpu.HBM),
        scratch_shapes=[
            pltpu.VMEM((lists, width), F32),
            pltpu.SemaphoreType.DMA((lists // CHUNK,)),
        ],
        compiler_params=params(),
        cost_estimate=pl.CostEstimate(flops=lists * width, bytes_accessed=8 * lists * width, transcendentals=0),
    )(numerators, mine, theirs)


def exchange(copies, axes):
    return lax.all_to_all(copies, axes, 0, 0, tiled=True)


def join_kernel(received_ref, copies_ref):
    copies_ref[...] = jnp.broadcast_to(jnp.sum(received_ref[...], axis=0)[None], copies_ref.shape)


def join(received, peers):
    return pl.pallas_call(
        join_kernel,
        out_shape=jax.ShapeDtypeStruct((peers,) + received.shape[1:], F32),
        in_specs=[IN_VMEM],
        out_specs=IN_VMEM,
        compiler_params=pltpu.CompilerParams(vmem_limit_bytes=1024 * 1024),
    )(received)


def sum_over_lists(copies):
    return exchange(join(exchange(copies, ("dp", "cx")), lax.axis_size("cz")), "cz")


def body(vectors, centroids):
    dp = lax.axis_size("dp")
    peers = dp * lax.axis_size("cx")
    lists_total = centroids.shape[0] * peers * lax.axis_size("cz")
    hops = (0, 2, 1, dp - 1)
    cx = lax.axis_size("cx")
    from_hop = lambda x, axis, hop, size: lax.ppermute(x, axis, [((i + hop) % size, i) for i in range(size)])
    share = unit_share(vectors, cx)
    far = from_hop(share, "dp", hops[1], dp)
    mine = unit_rows(vectors, share)
    unit_centroids = unit_lists(centroids)
    far, ready, unit_centroids = lax.optimization_barrier((far, mine, unit_centroids))
    near = [from_hop(ready, "dp", hop, dp) for hop in hops[2:]]
    shares = [far] + [from_hop(far, "cx", hop, cx) for hop in range(1, cx)]
    own = block_scores(unit_centroids, mine)
    far, far_kt = far_scores(unit_centroids, shares)
    kt, kt_sent, kept, sent, copies = first_sweep(
        unit_centroids, own, far_kt, [mine, far, *near], hops, lists_total, peers
    )
    swapped = lambda x: lax.ppermute(x, "replica", [(0, 1), (1, 0)])
    received = sum_over_lists(copies)
    received, kt_sent, sent = lax.optimization_barrier((received, kt_sent, sent))
    other_kt, other_vectors = swapped(kt_sent), swapped(sent)
    for sweep in range(1, ITERS):
        before = received
        copies, *scaled = next_sweep(before, kt, hops, lists_total, peers, sweep == ITERS - 1)
        if scaled:
            copies, other_before = lax.optimization_barrier((copies, swapped(before)))
        received = sum_over_lists(copies)
    other_received = swapped(received)
    own_numerators, other_scaled = own_update(
        received, scaled[0], kept, other_before, other_kt, hops, lists_total
    )
    numerators, squares = other_update(
        other_received, other_scaled, other_vectors, own_numerators, hops, lists_total
    )
    return finish(numerators, squares, swapped(squares))


def solution(mesh):
    cent = mesh.shape["cent"]
    split = Mesh(
        mesh.devices.reshape(mesh.shape["replica"], mesh.shape["dp"], 4, cent // 4),
        ("replica", "dp", "cx", "cz"),
    )
    placed = (P(("replica", "dp"), None), P(("dp", "cx", "cz"), None))
    return jax.shard_map(
        body, mesh=split, in_specs=placed, out_specs=P(("dp", "cx", "cz"), "replica"), check_vma=False
    )
```

```python
import functools
import math

import jax
import jax.numpy as jnp
from jax import lax
from jax.experimental import pallas as pl
from jax.experimental.pallas import tpu as pltpu
from jax.sharding import Mesh, PartitionSpec as P

VECTOR_WIDTH = 1024
ITERS = 3
SOFTMAX_HEAT = 0.05
EXPONENT = math.log2(math.e) / SOFTMAX_HEAT / VECTOR_WIDTH

LANES = 128
GROUP_ROWS = 8
CHUNK = 256
LONG = 512
TILE = 64
VMEM_LIMIT = 20 * 1024 * 1024
F32 = jnp.float32
BF16 = jnp.bfloat16

IN_VMEM = pl.BlockSpec(memory_space=pltpu.VMEM)


def params():
    return pltpu.CompilerParams(vmem_limit_bytes=VMEM_LIMIT)


def unit(values):
    scale = lax.rsqrt(jnp.mean(values * values, axis=-1, keepdims=True) + 1e-06)
    return (values * scale).astype(BF16)


def affinity(unit_centroids, unit_vectors):
    scores = lax.dot_general(
        unit_centroids, unit_vectors, (((1,), (1,)), ((), ())), preferred_element_type=F32
    )
    return jnp.exp2(scores * EXPONENT)


def share_kernel(values_ref, share_ref, rows_ref, sem):
    rows = share_ref.shape[0]
    first = pl.multiple_of(lax.axis_index("cx") * rows, rows)
    copy = pltpu.make_async_copy(values_ref.at[pl.ds(first, rows), :], rows_ref, sem)
    copy.start()
    copy.wait()
    share_ref[...] = unit(rows_ref[...])


def unit_share(values, shares):
    rows, width = values.shape[0] // shares, values.shape[1]
    return pl.pallas_call(
        share_kernel,
        out_shape=jax.ShapeDtypeStruct((rows, width), BF16),
        in_specs=[pl.BlockSpec(memory_space=pltpu.HBM)],
        out_specs=IN_VMEM,
        scratch_shapes=[pltpu.VMEM((rows, width), F32), pltpu.SemaphoreType.DMA(())],
        compiler_params=params(),
        cost_estimate=pl.CostEstimate(flops=4 * rows * width, bytes_accessed=6 * rows * width, transcendentals=0),
    )(pltpu.with_memory_space_constraint(values, pltpu.HBM))


def unit_kernel(values_ref, share_ref, unit_ref):
    unit_ref[...] = unit(values_ref[...])


def unit_rows(values, share):
    return pl.pallas_call(
        unit_kernel,
        out_shape=jax.ShapeDtypeStruct(values.shape, BF16),
        in_specs=[IN_VMEM, pl.BlockSpec(memory_space=pl.ANY)],
        out_specs=IN_VMEM,
        compiler_params=params(),
        cost_estimate=pl.CostEstimate(flops=4 * values.size, bytes_accessed=6 * values.size, transcendentals=0),
    )(values, share)


def stream_in(source_ref, held_ref, sems):
    copies = []
    for c, chunk in enumerate(chunks_of(source_ref.shape[0])):
        rows = pl.ds(chunk.start, CHUNK)
        copies.append(pltpu.make_async_copy(source_ref.at[rows, :], held_ref.at[rows, :], sems.at[c]))
        copies[-1].start()
    return copies


def centroids_kernel(centroids_ref, unit_ref, held_ref, sems):
    copies = stream_in(centroids_ref, held_ref, sems)
    for c, chunk in enumerate(chunks_of(centroids_ref.shape[0])):
        copies[c].wait()
        for t in range(chunk.start, chunk.stop, TILE):
            unit_ref[pl.ds(t, TILE), :] = unit(held_ref[pl.ds(t, TILE), :])


def unit_lists(centroids):
    lists, width = centroids.shape
    return pl.pallas_call(
        centroids_kernel,
        out_shape=jax.ShapeDtypeStruct((lists, width), BF16),
        in_specs=[pl.BlockSpec(memory_space=pltpu.HBM)],
        out_specs=IN_VMEM,
        scratch_shapes=[pltpu.VMEM((lists, width), F32), pltpu.SemaphoreType.DMA((lists // CHUNK,))],
        compiler_params=params(),
        cost_estimate=pl.CostEstimate(flops=4 * lists * width, bytes_accessed=6 * lists * width, transcendentals=0),
    )(pltpu.with_memory_space_constraint(centroids, pltpu.HBM))


def scaled_lists(kt, row_scale, lists_total):
    totals = jnp.sum(kt * row_scale, axis=1, keepdims=True)
    return kt * ((1.0 / lists_total) / totals)


def place_mass(mass, hops, rows_ref, copies_ref):
    row = jnp.sum(mass, axis=0, keepdims=True)
    blocks = len(hops)
    per_block = row.shape[1] // blocks // LANES
    here = lax.axis_index("dp")
    for j, hop in enumerate(hops):
        first = lax.rem(here + hop, blocks) * per_block
        for i in range(per_block):
            at = (j * per_block + i) * LANES
            rows_ref[pl.ds(first + i, 1), :] = row[:, at : at + LANES]
    copies_ref[...] = jnp.broadcast_to(rows_ref[...][None], copies_ref.shape)


def relative_row(rows_ref, hops):
    blocks = len(hops)
    per_block = rows_ref.shape[0] // blocks
    here = lax.axis_index("dp")
    parts = []
    for hop in hops:
        first = lax.rem(here + hop, blocks) * per_block
        parts += [rows_ref[pl.ds(first + i, 1), :] for i in range(per_block)]
    return jnp.concatenate(parts, axis=1)


def sweep_lists(kt_ref, row_scale, lists, lists_total, scaled_ref=None):
    mass = jnp.zeros((GROUP_ROWS, kt_ref.shape[1]), F32)
    for t in range(lists.start, lists.stop, TILE):
        scaled = scaled_lists(kt_ref[pl.ds(t, TILE), :], row_scale, lists_total)
        mass = mass + jnp.sum(scaled.reshape(-1, GROUP_ROWS, scaled.shape[1]), axis=0)
        if scaled_ref is not None:
            scaled_ref[pl.ds(t, TILE), :] = scaled
    return mass


def chunks_of(lists, size=CHUNK):
    return [range(at, at + size) for at in range(0, lists, size)]


def score_lists(centroids_ref, vectors_ref, scores_ref):
    for chunk in chunks_of(scores_ref.shape[0], LONG):
        rows = pl.ds(chunk.start, LONG)
        scores_ref[rows, :] = affinity(centroids_ref[rows, :], vectors_ref[...])


def far_kernel(centroids_ref, *refs):
    *share_refs, vectors_ref, scores_ref = refs
    for j, share_ref in enumerate(share_refs):
        rows = share_ref.shape[0]
        at = lax.rem(lax.axis_index("cx") + j, len(share_refs)) * rows
        vectors_ref[pl.ds(pl.multiple_of(at, rows), rows), :] = share_ref[...]
    score_lists(centroids_ref, vectors_ref, scores_ref)


def score_cost(lists, width, columns):
    return pl.CostEstimate(
        flops=2 * lists * width * columns, bytes_accessed=4 * lists * width, transcendentals=lists * columns
    )


def block_scores(unit_centroids, vectors):
    lists, width = unit_centroids.shape
    block = vectors.shape[0]
    return pl.pallas_call(
        score_lists,
        out_shape=jax.ShapeDtypeStruct((lists, block), F32),
        in_specs=[IN_VMEM] * 2,
        out_specs=IN_VMEM,
        compiler_params=params(),
        cost_estimate=score_cost(lists, width, block),
    )(unit_centroids, vectors)


def far_scores(unit_centroids, shares):
    lists, width = unit_centroids.shape
    block = shares[0].shape[0] * len(shares)
    return pl.pallas_call(
        far_kernel,
        out_shape=(jax.ShapeDtypeStruct((block, width), BF16), jax.ShapeDtypeStruct((lists, block), F32)),
        in_specs=[IN_VMEM] * (1 + len(shares)),
        out_specs=(IN_VMEM, IN_VMEM),
        compiler_params=params(),
        cost_estimate=score_cost(lists, width, block),
    )(unit_centroids, *shares)


def first_kernel(hops, lists_total, centroids_ref, own_ref, far_ref, *refs):
    blocks = len(hops)
    vector_refs = refs[:blocks]
    kt_ref, kt_send_ref, keep_ref, send_ref, copies_ref, slab_ref, rows_ref, sems = refs[blocks:]
    lists, slab = kt_ref.shape
    block = own_ref.shape[1]
    known = block + far_ref.shape[1]
    for j, vector_ref in enumerate(vector_refs):
        slab_ref[pl.ds(j * block, block), :] = vector_ref[...]
    half = keep_ref.shape[1]
    here = lax.axis_index("replica")
    keep_ref[...] = slab_ref[:, pl.ds(pl.multiple_of(here * half, half), half)]
    send_ref[...] = slab_ref[:, pl.ds(pl.multiple_of((1 - here) * half, half), half)]
    row_scale = jnp.full((1, slab), 1.0 / slab, F32)
    sends = []
    for c, chunk in enumerate(chunks_of(lists)):
        rows = pl.ds(chunk.start, CHUNK)
        kt_ref[rows, :block] = own_ref[rows, :]
        kt_ref[rows, block:known] = far_ref[rows, :]
        kt_ref[rows, known:] = affinity(centroids_ref[rows, :], slab_ref[known:, :])
        sends.append(pltpu.make_async_copy(kt_ref.at[rows, :], kt_send_ref.at[rows, :], sems.at[c]))
        sends[-1].start()
    mass = sweep_lists(kt_ref, row_scale, range(lists), lists_total)
    place_mass(mass, hops, rows_ref, copies_ref)
    for send in sends:
        send.wait()


def first_sweep(unit_centroids, own, far, vectors, hops, lists_total, peers):
    lists, width = unit_centroids.shape
    slab = own.shape[1] * len(hops)
    rows = slab // LANES
    return pl.pallas_call(
        functools.partial(first_kernel, hops, lists_total),
        out_shape=(
            jax.ShapeDtypeStruct((lists, slab), F32),
            pltpu.HBM((lists, slab), F32),
            *[jax.ShapeDtypeStruct((slab, width // 2), BF16)] * 2,
            jax.ShapeDtypeStruct((peers, rows, LANES), F32),
        ),
        in_specs=[IN_VMEM] * (3 + len(vectors)),
        out_specs=(IN_VMEM, pl.BlockSpec(memory_space=pltpu.HBM), IN_VMEM, IN_VMEM, IN_VMEM),
        scratch_shapes=[
            pltpu.VMEM((slab, width), BF16),
            pltpu.VMEM((rows, LANES), F32),
            pltpu.SemaphoreType.DMA((lists // CHUNK,)),
        ],
        compiler_params=params(),
        cost_estimate=pl.CostEstimate(
            flops=lists * width * slab, bytes_accessed=6 * lists * slab, transcendentals=lists * slab // 2
        ),
    )(unit_centroids, own, far, *vectors)


def row_scale_of(received_ref, rows_ref, hops):
    totals = jnp.sum(received_ref[...], axis=0)
    rows_ref[...] = (1.0 / (totals.shape[0] * totals.shape[1])) / totals
    return relative_row(rows_ref, hops)


def sweep_kernel(hops, lists_total, received_ref, kt_ref, copies_ref, *refs):
    *scaled_refs, rows_ref = refs
    row_scale = row_scale_of(received_ref, rows_ref, hops)
    mass = sweep_lists(kt_ref, row_scale, range(kt_ref.shape[0]), lists_total, *scaled_refs)
    place_mass(mass, hops, rows_ref, copies_ref)


def next_sweep(received, kt, hops, lists_total, peers, last):
    lists, slab = kt.shape
    rows = slab // LANES
    outs = [jax.ShapeDtypeStruct((peers, rows, LANES), F32)] + [jax.ShapeDtypeStruct((lists, slab), F32)] * last
    return pl.pallas_call(
        functools.partial(sweep_kernel, hops, lists_total),
        out_shape=outs,
        in_specs=[IN_VMEM] * 2,
        out_specs=[IN_VMEM] * len(outs),
        scratch_shapes=[pltpu.VMEM((rows, LANES), F32)],
        compiler_params=params(),
        cost_estimate=pl.CostEstimate(flops=4 * lists * slab, bytes_accessed=4 * lists * slab, transcendentals=0),
    )(received, kt)


def to_row(column):
    return jnp.broadcast_to(column, (LANES, LANES)).T[:1, :]


def to_lanes(row):
    return jnp.broadcast_to(row, (LANES, LANES)).T


def write_weights(scaled_ref, scale, weights_ref, lists):
    for t in range(lists.start, lists.stop, TILE):
        weights_ref[pl.ds(t, TILE), :] = (scaled_ref[pl.ds(t, TILE), :] * scale).astype(BF16)


def own_update_kernel(
    hops, lists_total, received_ref, scaled_ref, slab_ref, other_before_ref, other_kt_ref,
    out_ref, other_scaled_ref, weights_ref, rows_ref, sems,
):
    lists, slab = scaled_ref.shape
    copies = stream_in(other_kt_ref, other_scaled_ref, sems)
    scale = row_scale_of(received_ref, rows_ref, hops) * (slab * lists_total)
    other_before_scale = row_scale_of(other_before_ref, rows_ref, hops)
    for chunk in chunks_of(lists, LONG):
        rows = pl.ds(chunk.start, LONG)
        write_weights(scaled_ref, scale, weights_ref, chunk)
        out_ref[rows, :] = jnp.dot(weights_ref[rows, :], slab_ref[...], preferred_element_type=F32)
    for c, chunk in enumerate(chunks_of(lists)):
        copies[c].wait()
        for t in range(chunk.start, chunk.stop, TILE):
            rows = pl.ds(t, TILE)
            other_scaled_ref[rows, :] = scaled_lists(other_scaled_ref[rows, :], other_before_scale, lists_total)


def own_update(received, scaled, slab_vectors, other_before, other_kt, hops, lists_total):
    lists, slab = scaled.shape
    width = slab_vectors.shape[1]
    return pl.pallas_call(
        functools.partial(own_update_kernel, hops, lists_total),
        out_shape=(jax.ShapeDtypeStruct((lists, width), F32), jax.ShapeDtypeStruct((lists, slab), F32)),
        in_specs=[IN_VMEM] * 4 + [pl.BlockSpec(memory_space=pltpu.HBM)],
        out_specs=(IN_VMEM, IN_VMEM),
        scratch_shapes=[
            pltpu.VMEM((lists, slab), BF16),
            pltpu.VMEM((slab // LANES, LANES), F32),
            pltpu.SemaphoreType.DMA((lists // CHUNK,)),
        ],
        compiler_params=params(),
        cost_estimate=pl.CostEstimate(
            flops=2 * lists * width * slab, bytes_accessed=6 * lists * slab, transcendentals=0
        ),
    )(received, scaled, slab_vectors, other_before, other_kt)


def other_update_kernel(
    hops, lists_total, received_ref, scaled_ref, slab_ref, earlier_ref,
    total_ref, squares_ref, weights_ref, rows_ref,
):
    lists, slab = scaled_ref.shape
    scale = row_scale_of(received_ref, rows_ref, hops) * (slab * lists_total)
    for chunk in chunks_of(lists, LONG):
        rows = pl.ds(chunk.start, LONG)
        write_weights(scaled_ref, scale, weights_ref, chunk)
        total = jnp.dot(weights_ref[rows, :], slab_ref[...], preferred_element_type=F32)
        total = total + earlier_ref[rows, :]
        total_ref[rows, :] = total
        squares = jnp.sum(total * total, axis=1, keepdims=True)
        for k in range(LONG // LANES):
            at = chunk.start // LANES + k
            squares_ref[at : at + 1, :] = to_row(squares[k * LANES : (k + 1) * LANES])


def other_update(received, scaled, slab_vectors, earlier, hops, lists_total):
    lists, slab = scaled.shape
    width = slab_vectors.shape[1]
    return pl.pallas_call(
        functools.partial(other_update_kernel, hops, lists_total),
        out_shape=(
            jax.ShapeDtypeStruct((lists, width), F32),
            jax.ShapeDtypeStruct((lists // LANES, LANES), F32),
        ),
        in_specs=[IN_VMEM] * 4,
        out_specs=(IN_VMEM, IN_VMEM),
        scratch_shapes=[pltpu.VMEM((lists, slab), BF16), pltpu.VMEM((slab // LANES, LANES), F32)],
        compiler_params=params(),
        cost_estimate=pl.CostEstimate(
            flops=2 * lists * width * slab, bytes_accessed=8 * lists * slab, transcendentals=0
        ),
    )(received, scaled, slab_vectors, earlier)


def finish_kernel(numerators_ref, mine_ref, theirs_ref, out_ref, scaled_ref, sems):
    lists, width = numerators_ref.shape
    scales = lax.rsqrt((mine_ref[...] + theirs_ref[...]) / VECTOR_WIDTH + 1e-06)
    copies = []
    for c, chunk in enumerate(chunks_of(lists)):
        for k in range(CHUNK // LANES):
            at = chunk.start + k * LANES
            scale = to_lanes(scales[at // LANES : at // LANES + 1, :])
            for f in range(0, width, LANES):
                scaled_ref[at : at + LANES, f : f + LANES] = numerators_ref[at : at + LANES, f : f + LANES] * scale
        rows = pl.ds(chunk.start, CHUNK)
        copies.append(pltpu.make_async_copy(scaled_ref.at[rows, :], out_ref.at[rows, :], sems.at[c]))
        copies[-1].start()
    for copy in copies:
        copy.wait()


def finish(numerators, mine, theirs):
    lists, width = numerators.shape
    return pl.pallas_call(
        finish_kernel,
        out_shape=jax.ShapeDtypeStruct((lists, width), F32),
        in_specs=[IN_VMEM] * 3,
        out_specs=pl.BlockSpec(memory_space=pltpu.HBM),
        scratch_shapes=[
            pltpu.VMEM((lists, width), F32),
            pltpu.SemaphoreType.DMA((lists // CHUNK,)),
        ],
        compiler_params=params(),
        cost_estimate=pl.CostEstimate(flops=lists * width, bytes_accessed=8 * lists * width, transcendentals=0),
    )(numerators, mine, theirs)


def exchange(copies, axes):
    return lax.all_to_all(copies, axes, 0, 0, tiled=True)


def join_kernel(received_ref, copies_ref):
    copies_ref[...] = jnp.broadcast_to(jnp.sum(received_ref[...], axis=0)[None], copies_ref.shape)


def join(received, peers):
    return pl.pallas_call(
        join_kernel,
        out_shape=jax.ShapeDtypeStruct((peers,) + received.shape[1:], F32),
        in_specs=[IN_VMEM],
        out_specs=IN_VMEM,
        compiler_params=pltpu.CompilerParams(vmem_limit_bytes=1024 * 1024),
    )(received)


def sum_over_lists(copies):
    return exchange(join(exchange(copies, ("dp", "cx")), lax.axis_size("cz")), "cz")


def body(vectors, centroids):
    dp = lax.axis_size("dp")
    peers = dp * lax.axis_size("cx")
    lists_total = centroids.shape[0] * peers * lax.axis_size("cz")
    hops = (0, 2, 1, dp - 1)
    cx = lax.axis_size("cx")
    from_hop = lambda x, axis, hop, size: lax.ppermute(x, axis, [((i + hop) % size, i) for i in range(size)])
    share = unit_share(vectors, cx)
    far = from_hop(share, "dp", hops[1], dp)
    mine = unit_rows(vectors, share)
    unit_centroids = unit_lists(centroids)
    far, ready, unit_centroids = lax.optimization_barrier((far, mine, unit_centroids))
    near = [from_hop(ready, "dp", hop, dp) for hop in hops[2:]]
    shares = [far] + [from_hop(far, "cx", hop, cx) for hop in range(1, cx)]
    own = block_scores(unit_centroids, mine)
    far, far_kt = far_scores(unit_centroids, shares)
    kt, kt_sent, kept, sent, copies = first_sweep(
        unit_centroids, own, far_kt, [mine, far, *near], hops, lists_total, peers
    )
    swapped = lambda x: lax.ppermute(x, "replica", [(0, 1), (1, 0)])
    received = sum_over_lists(copies)
    received, kt_sent, sent = lax.optimization_barrier((received, kt_sent, sent))
    other_kt, other_vectors = swapped(kt_sent), swapped(sent)
    for sweep in range(1, ITERS):
        before = received
        copies, *scaled = next_sweep(before, kt, hops, lists_total, peers, sweep == ITERS - 1)
        if scaled:
            copies, other_before = lax.optimization_barrier((copies, swapped(before)))
        received = sum_over_lists(copies)
    other_received = swapped(received)
    own_numerators, other_scaled = own_update(
        received, scaled[0], kept, other_before, other_kt, hops, lists_total
    )
    numerators, squares = other_update(
        other_received, other_scaled, other_vectors, own_numerators, hops, lists_total
    )
    return finish(numerators, squares, swapped(squares))


def solution(mesh):
    cent = mesh.shape["cent"]
    split = Mesh(
        mesh.devices.reshape(mesh.shape["replica"], mesh.shape["dp"], 4, cent // 4),
        ("replica", "dp", "cx", "cz"),
    )
    placed = (P(("replica", "dp"), None), P(("dp", "cx", "cz"), None))
    return jax.shard_map(
        body, mesh=split, in_specs=placed, out_specs=P(("dp", "cx", "cz"), "replica"), check_vma=False
    )
```

```python
import functools
import math

import jax
import jax.numpy as jnp
from jax import lax
from jax.experimental import pallas as pl
from jax.experimental.pallas import tpu as pltpu
from jax.sharding import Mesh, PartitionSpec as P

VECTOR_WIDTH = 1024
ITERS = 3
SOFTMAX_HEAT = 0.05
EXPONENT = math.log2(math.e) / SOFTMAX_HEAT / VECTOR_WIDTH

LANES = 128
GROUP_ROWS = 8
CHUNK = 256
LONG = 512
TILE = 32
VMEM_LIMIT = 20 * 1024 * 1024
F32 = jnp.float32
BF16 = jnp.bfloat16

IN_VMEM = pl.BlockSpec(memory_space=pltpu.VMEM)


def params():
    return pltpu.CompilerParams(vmem_limit_bytes=VMEM_LIMIT)


def unit(values):
    scale = lax.rsqrt(jnp.mean(values * values, axis=-1, keepdims=True) + 1e-06)
    return (values * scale).astype(BF16)


def affinity(unit_centroids, unit_vectors):
    scores = lax.dot_general(
        unit_centroids, unit_vectors, (((1,), (1,)), ((), ())), preferred_element_type=F32
    )
    return jnp.exp2(scores * EXPONENT)


def share_kernel(values_ref, share_ref, rows_ref, sem):
    rows = share_ref.shape[0]
    first = pl.multiple_of(lax.axis_index("cx") * rows, rows)
    copy = pltpu.make_async_copy(values_ref.at[pl.ds(first, rows), :], rows_ref, sem)
    copy.start()
    copy.wait()
    share_ref[...] = unit(rows_ref[...])


def unit_share(values, shares):
    rows, width = values.shape[0] // shares, values.shape[1]
    return pl.pallas_call(
        share_kernel,
        out_shape=jax.ShapeDtypeStruct((rows, width), BF16),
        in_specs=[pl.BlockSpec(memory_space=pltpu.HBM)],
        out_specs=IN_VMEM,
        scratch_shapes=[pltpu.VMEM((rows, width), F32), pltpu.SemaphoreType.DMA(())],
        compiler_params=params(),
        cost_estimate=pl.CostEstimate(flops=4 * rows * width, bytes_accessed=6 * rows * width, transcendentals=0),
    )(pltpu.with_memory_space_constraint(values, pltpu.HBM))


def unit_kernel(values_ref, share_ref, unit_ref):
    unit_ref[...] = unit(values_ref[...])


def unit_rows(values, share):
    return pl.pallas_call(
        unit_kernel,
        out_shape=jax.ShapeDtypeStruct(values.shape, BF16),
        in_specs=[IN_VMEM, pl.BlockSpec(memory_space=pl.ANY)],
        out_specs=IN_VMEM,
        compiler_params=params(),
        cost_estimate=pl.CostEstimate(flops=4 * values.size, bytes_accessed=6 * values.size, transcendentals=0),
    )(values, share)


def stream_in(source_ref, held_ref, sems):
    copies = []
    for c, chunk in enumerate(chunks_of(source_ref.shape[0])):
        rows = pl.ds(chunk.start, CHUNK)
        copies.append(pltpu.make_async_copy(source_ref.at[rows, :], held_ref.at[rows, :], sems.at[c]))
        copies[-1].start()
    return copies


def centroids_kernel(centroids_ref, unit_ref, held_ref, sems):
    copies = stream_in(centroids_ref, held_ref, sems)
    for c, chunk in enumerate(chunks_of(centroids_ref.shape[0])):
        copies[c].wait()
        for t in range(chunk.start, chunk.stop, TILE):
            unit_ref[pl.ds(t, TILE), :] = unit(held_ref[pl.ds(t, TILE), :])


def unit_lists(centroids):
    lists, width = centroids.shape
    return pl.pallas_call(
        centroids_kernel,
        out_shape=jax.ShapeDtypeStruct((lists, width), BF16),
        in_specs=[pl.BlockSpec(memory_space=pltpu.HBM)],
        out_specs=IN_VMEM,
        scratch_shapes=[pltpu.VMEM((lists, width), F32), pltpu.SemaphoreType.DMA((lists // CHUNK,))],
        compiler_params=params(),
        cost_estimate=pl.CostEstimate(flops=4 * lists * width, bytes_accessed=6 * lists * width, transcendentals=0),
    )(pltpu.with_memory_space_constraint(centroids, pltpu.HBM))


def scaled_lists(kt, row_scale, lists_total):
    totals = jnp.sum(kt * row_scale, axis=1, keepdims=True)
    return kt * ((1.0 / lists_total) / totals)


def place_mass(mass, hops, rows_ref, copies_ref):
    row = jnp.sum(mass, axis=0, keepdims=True)
    blocks = len(hops)
    per_block = row.shape[1] // blocks // LANES
    here = lax.axis_index("dp")
    for j, hop in enumerate(hops):
        first = lax.rem(here + hop, blocks) * per_block
        for i in range(per_block):
            at = (j * per_block + i) * LANES
            rows_ref[pl.ds(first + i, 1), :] = row[:, at : at + LANES]
    copies_ref[...] = jnp.broadcast_to(rows_ref[...][None], copies_ref.shape)


def relative_row(rows_ref, hops):
    blocks = len(hops)
    per_block = rows_ref.shape[0] // blocks
    here = lax.axis_index("dp")
    parts = []
    for hop in hops:
        first = lax.rem(here + hop, blocks) * per_block
        parts += [rows_ref[pl.ds(first + i, 1), :] for i in range(per_block)]
    return jnp.concatenate(parts, axis=1)


def sweep_lists(kt_ref, row_scale, lists, lists_total, scaled_ref=None):
    mass = jnp.zeros((GROUP_ROWS, kt_ref.shape[1]), F32)
    for t in range(lists.start, lists.stop, TILE):
        scaled = scaled_lists(kt_ref[pl.ds(t, TILE), :], row_scale, lists_total)
        mass = mass + jnp.sum(scaled.reshape(-1, GROUP_ROWS, scaled.shape[1]), axis=0)
        if scaled_ref is not None:
            scaled_ref[pl.ds(t, TILE), :] = scaled
    return mass


def chunks_of(lists, size=CHUNK):
    return [range(at, at + size) for at in range(0, lists, size)]


def score_lists(centroids_ref, vectors_ref, scores_ref):
    for chunk in chunks_of(scores_ref.shape[0], LONG):
        rows = pl.ds(chunk.start, LONG)
        scores_ref[rows, :] = affinity(centroids_ref[rows, :], vectors_ref[...])


def far_kernel(centroids_ref, *refs):
    *share_refs, vectors_ref, scores_ref = refs
    for j, share_ref in enumerate(share_refs):
        rows = share_ref.shape[0]
        at = lax.rem(lax.axis_index("cx") + j, len(share_refs)) * rows
        vectors_ref[pl.ds(pl.multiple_of(at, rows), rows), :] = share_ref[...]
    score_lists(centroids_ref, vectors_ref, scores_ref)


def score_cost(lists, width, columns):
    return pl.CostEstimate(
        flops=2 * lists * width * columns, bytes_accessed=4 * lists * width, transcendentals=lists * columns
    )


def block_scores(unit_centroids, vectors):
    lists, width = unit_centroids.shape
    block = vectors.shape[0]
    return pl.pallas_call(
        score_lists,
        out_shape=jax.ShapeDtypeStruct((lists, block), F32),
        in_specs=[IN_VMEM] * 2,
        out_specs=IN_VMEM,
        compiler_params=params(),
        cost_estimate=score_cost(lists, width, block),
    )(unit_centroids, vectors)


def far_scores(unit_centroids, shares):
    lists, width = unit_centroids.shape
    block = shares[0].shape[0] * len(shares)
    return pl.pallas_call(
        far_kernel,
        out_shape=(jax.ShapeDtypeStruct((block, width), BF16), jax.ShapeDtypeStruct((lists, block), F32)),
        in_specs=[IN_VMEM] * (1 + len(shares)),
        out_specs=(IN_VMEM, IN_VMEM),
        compiler_params=params(),
        cost_estimate=score_cost(lists, width, block),
    )(unit_centroids, *shares)


def first_kernel(hops, lists_total, centroids_ref, own_ref, far_ref, *refs):
    blocks = len(hops)
    vector_refs = refs[:blocks]
    kt_ref, kt_send_ref, keep_ref, send_ref, copies_ref, slab_ref, rows_ref, sems = refs[blocks:]
    lists, slab = kt_ref.shape
    block = own_ref.shape[1]
    known = block + far_ref.shape[1]
    for j, vector_ref in enumerate(vector_refs):
        slab_ref[pl.ds(j * block, block), :] = vector_ref[...]
    half = keep_ref.shape[1]
    here = lax.axis_index("replica")
    keep_ref[...] = slab_ref[:, pl.ds(pl.multiple_of(here * half, half), half)]
    send_ref[...] = slab_ref[:, pl.ds(pl.multiple_of((1 - here) * half, half), half)]
    row_scale = jnp.full((1, slab), 1.0 / slab, F32)
    mass = jnp.zeros((GROUP_ROWS, slab), F32)
    sends = []
    for c, chunk in enumerate(chunks_of(lists, LONG)):
        rows = pl.ds(chunk.start, LONG)
        kt_ref[rows, :block] = own_ref[rows, :]
        kt_ref[rows, block:known] = far_ref[rows, :]
        kt_ref[rows, known:] = affinity(centroids_ref[rows, :], slab_ref[known:, :])
        sends.append(pltpu.make_async_copy(kt_ref.at[rows, :], kt_send_ref.at[rows, :], sems.at[c]))
        sends[-1].start()
        mass = mass + sweep_lists(kt_ref, row_scale, chunk, lists_total)
    place_mass(mass, hops, rows_ref, copies_ref)
    for send in sends:
        send.wait()


def first_sweep(unit_centroids, own, far, vectors, hops, lists_total, peers):
    lists, width = unit_centroids.shape
    slab = own.shape[1] * len(hops)
    rows = slab // LANES
    return pl.pallas_call(
        functools.partial(first_kernel, hops, lists_total),
        out_shape=(
            jax.ShapeDtypeStruct((lists, slab), F32),
            pltpu.HBM((lists, slab), F32),
            *[jax.ShapeDtypeStruct((slab, width // 2), BF16)] * 2,
            jax.ShapeDtypeStruct((peers, rows, LANES), F32),
        ),
        in_specs=[IN_VMEM] * (3 + len(vectors)),
        out_specs=(IN_VMEM, pl.BlockSpec(memory_space=pltpu.HBM), IN_VMEM, IN_VMEM, IN_VMEM),
        scratch_shapes=[
            pltpu.VMEM((slab, width), BF16),
            pltpu.VMEM((rows, LANES), F32),
            pltpu.SemaphoreType.DMA((lists // LONG,)),
        ],
        compiler_params=params(),
        cost_estimate=pl.CostEstimate(
            flops=lists * width * slab, bytes_accessed=6 * lists * slab, transcendentals=lists * slab // 2
        ),
    )(unit_centroids, own, far, *vectors)


def row_scale_of(received_ref, rows_ref, hops):
    totals = jnp.sum(received_ref[...], axis=0)
    rows_ref[...] = (1.0 / (totals.shape[0] * totals.shape[1])) / totals
    return relative_row(rows_ref, hops)


def sweep_kernel(hops, lists_total, received_ref, kt_ref, copies_ref, *refs):
    *scaled_refs, rows_ref = refs
    row_scale = row_scale_of(received_ref, rows_ref, hops)
    mass = sweep_lists(kt_ref, row_scale, range(kt_ref.shape[0]), lists_total, *scaled_refs)
    place_mass(mass, hops, rows_ref, copies_ref)


def next_sweep(received, kt, hops, lists_total, peers, last):
    lists, slab = kt.shape
    rows = slab // LANES
    outs = [jax.ShapeDtypeStruct((peers, rows, LANES), F32)] + [jax.ShapeDtypeStruct((lists, slab), F32)] * last
    return pl.pallas_call(
        functools.partial(sweep_kernel, hops, lists_total),
        out_shape=outs,
        in_specs=[IN_VMEM] * 2,
        out_specs=[IN_VMEM] * len(outs),
        scratch_shapes=[pltpu.VMEM((rows, LANES), F32)],
        compiler_params=params(),
        cost_estimate=pl.CostEstimate(flops=4 * lists * slab, bytes_accessed=4 * lists * slab, transcendentals=0),
    )(received, kt)


def to_row(column):
    return jnp.broadcast_to(column, (LANES, LANES)).T[:1, :]


def to_lanes(row):
    return jnp.broadcast_to(row, (LANES, LANES)).T


def write_weights(scaled_ref, scale, weights_ref, lists):
    for t in range(lists.start, lists.stop, TILE):
        weights_ref[pl.ds(t, TILE), :] = (scaled_ref[pl.ds(t, TILE), :] * scale).astype(BF16)


def own_update_kernel(
    hops, lists_total, received_ref, scaled_ref, slab_ref, other_before_ref, other_kt_ref,
    out_ref, other_scaled_ref, weights_ref, rows_ref, sems,
):
    lists, slab = scaled_ref.shape
    copies = stream_in(other_kt_ref, other_scaled_ref, sems)
    scale = row_scale_of(received_ref, rows_ref, hops) * (slab * lists_total)
    other_before_scale = row_scale_of(other_before_ref, rows_ref, hops)
    for chunk in chunks_of(lists, LONG):
        rows = pl.ds(chunk.start, LONG)
        write_weights(scaled_ref, scale, weights_ref, chunk)
        out_ref[rows, :] = jnp.dot(weights_ref[rows, :], slab_ref[...], preferred_element_type=F32)
    for c, chunk in enumerate(chunks_of(lists)):
        copies[c].wait()
        for t in range(chunk.start, chunk.stop, TILE):
            rows = pl.ds(t, TILE)
            other_scaled_ref[rows, :] = scaled_lists(other_scaled_ref[rows, :], other_before_scale, lists_total)


def own_update(received, scaled, slab_vectors, other_before, other_kt, hops, lists_total):
    lists, slab = scaled.shape
    width = slab_vectors.shape[1]
    return pl.pallas_call(
        functools.partial(own_update_kernel, hops, lists_total),
        out_shape=(jax.ShapeDtypeStruct((lists, width), F32), jax.ShapeDtypeStruct((lists, slab), F32)),
        in_specs=[IN_VMEM] * 4 + [pl.BlockSpec(memory_space=pltpu.HBM)],
        out_specs=(IN_VMEM, IN_VMEM),
        scratch_shapes=[
            pltpu.VMEM((lists, slab), BF16),
            pltpu.VMEM((slab // LANES, LANES), F32),
            pltpu.SemaphoreType.DMA((lists // CHUNK,)),
        ],
        compiler_params=params(),
        cost_estimate=pl.CostEstimate(
            flops=2 * lists * width * slab, bytes_accessed=6 * lists * slab, transcendentals=0
        ),
    )(received, scaled, slab_vectors, other_before, other_kt)


def other_update_kernel(
    hops, lists_total, received_ref, scaled_ref, slab_ref, earlier_ref,
    total_ref, squares_ref, weights_ref, rows_ref,
):
    lists, slab = scaled_ref.shape
    scale = row_scale_of(received_ref, rows_ref, hops) * (slab * lists_total)
    for chunk in chunks_of(lists, LONG):
        rows = pl.ds(chunk.start, LONG)
        write_weights(scaled_ref, scale, weights_ref, chunk)
        total = jnp.dot(weights_ref[rows, :], slab_ref[...], preferred_element_type=F32)
        total = total + earlier_ref[rows, :]
        total_ref[rows, :] = total
        squares = jnp.sum(total * total, axis=1, keepdims=True)
        for k in range(LONG // LANES):
            at = chunk.start // LANES + k
            squares_ref[at : at + 1, :] = to_row(squares[k * LANES : (k + 1) * LANES])


def other_update(received, scaled, slab_vectors, earlier, hops, lists_total):
    lists, slab = scaled.shape
    width = slab_vectors.shape[1]
    return pl.pallas_call(
        functools.partial(other_update_kernel, hops, lists_total),
        out_shape=(
            jax.ShapeDtypeStruct((lists, width), F32),
            jax.ShapeDtypeStruct((lists // LANES, LANES), F32),
        ),
        in_specs=[IN_VMEM] * 4,
        out_specs=(IN_VMEM, IN_VMEM),
        scratch_shapes=[pltpu.VMEM((lists, slab), BF16), pltpu.VMEM((slab // LANES, LANES), F32)],
        compiler_params=params(),
        cost_estimate=pl.CostEstimate(
            flops=2 * lists * width * slab, bytes_accessed=8 * lists * slab, transcendentals=0
        ),
    )(received, scaled, slab_vectors, earlier)


def finish_kernel(numerators_ref, mine_ref, theirs_ref, out_ref, scaled_ref, sems):
    lists, width = numerators_ref.shape
    scales = lax.rsqrt((mine_ref[...] + theirs_ref[...]) / VECTOR_WIDTH + 1e-06)
    copies = []
    for c, chunk in enumerate(chunks_of(lists)):
        for k in range(CHUNK // LANES):
            at = chunk.start + k * LANES
            scale = to_lanes(scales[at // LANES : at // LANES + 1, :])
            for f in range(0, width, LANES):
                scaled_ref[at : at + LANES, f : f + LANES] = numerators_ref[at : at + LANES, f : f + LANES] * scale
        rows = pl.ds(chunk.start, CHUNK)
        copies.append(pltpu.make_async_copy(scaled_ref.at[rows, :], out_ref.at[rows, :], sems.at[c]))
        copies[-1].start()
    for copy in copies:
        copy.wait()


def finish(numerators, mine, theirs):
    lists, width = numerators.shape
    return pl.pallas_call(
        finish_kernel,
        out_shape=jax.ShapeDtypeStruct((lists, width), F32),
        in_specs=[IN_VMEM] * 3,
        out_specs=pl.BlockSpec(memory_space=pltpu.HBM),
        scratch_shapes=[
            pltpu.VMEM((lists, width), F32),
            pltpu.SemaphoreType.DMA((lists // CHUNK,)),
        ],
        compiler_params=params(),
        cost_estimate=pl.CostEstimate(flops=lists * width, bytes_accessed=8 * lists * width, transcendentals=0),
    )(numerators, mine, theirs)


def exchange(copies, axes):
    return lax.all_to_all(copies, axes, 0, 0, tiled=True)


def join_kernel(received_ref, copies_ref):
    copies_ref[...] = jnp.broadcast_to(jnp.sum(received_ref[...], axis=0)[None], copies_ref.shape)


def join(received, peers):
    return pl.pallas_call(
        join_kernel,
        out_shape=jax.ShapeDtypeStruct((peers,) + received.shape[1:], F32),
        in_specs=[IN_VMEM],
        out_specs=IN_VMEM,
        compiler_params=pltpu.CompilerParams(vmem_limit_bytes=1024 * 1024),
    )(received)


def sum_over_lists(copies):
    return exchange(join(exchange(copies, ("dp", "cx")), lax.axis_size("cz")), "cz")


def body(vectors, centroids):
    dp = lax.axis_size("dp")
    peers = dp * lax.axis_size("cx")
    lists_total = centroids.shape[0] * peers * lax.axis_size("cz")
    hops = (0, 2, 1, dp - 1)
    cx = lax.axis_size("cx")
    from_hop = lambda x, axis, hop, size: lax.ppermute(x, axis, [((i + hop) % size, i) for i in range(size)])
    share = unit_share(vectors, cx)
    far = from_hop(share, "dp", hops[1], dp)
    mine = unit_rows(vectors, share)
    unit_centroids = unit_lists(centroids)
    far, ready, unit_centroids = lax.optimization_barrier((far, mine, unit_centroids))
    near = [from_hop(ready, "dp", hop, dp) for hop in hops[2:]]
    shares = [far] + [from_hop(far, "cx", hop, cx) for hop in range(1, cx)]
    own = block_scores(unit_centroids, mine)
    far, far_kt = far_scores(unit_centroids, shares)
    kt, kt_sent, kept, sent, copies = first_sweep(
        unit_centroids, own, far_kt, [mine, far, *near], hops, lists_total, peers
    )
    swapped = lambda x: lax.ppermute(x, "replica", [(0, 1), (1, 0)])
    received = sum_over_lists(copies)
    received, kt_sent, sent = lax.optimization_barrier((received, kt_sent, sent))
    other_kt, other_vectors = swapped(kt_sent), swapped(sent)
    for sweep in range(1, ITERS):
        before = received
        copies, *scaled = next_sweep(before, kt, hops, lists_total, peers, sweep == ITERS - 1)
        if scaled:
            copies, other_before = lax.optimization_barrier((copies, swapped(before)))
        received = sum_over_lists(copies)
    other_received = swapped(received)
    own_numerators, other_scaled = own_update(
        received, scaled[0], kept, other_before, other_kt, hops, lists_total
    )
    numerators, squares = other_update(
        other_received, other_scaled, other_vectors, own_numerators, hops, lists_total
    )
    return finish(numerators, squares, swapped(squares))


def solution(mesh):
    cent = mesh.shape["cent"]
    split = Mesh(
        mesh.devices.reshape(mesh.shape["replica"], mesh.shape["dp"], 4, cent // 4),
        ("replica", "dp", "cx", "cz"),
    )
    placed = (P(("replica", "dp"), None), P(("dp", "cx", "cz"), None))
    return jax.shard_map(
        body, mesh=split, in_specs=placed, out_specs=P(("dp", "cx", "cz"), "replica"), check_vma=False
    )
```
